512 devices in a mesh: rows: 128 (over z, y, core), modes: 4 (over x).
Axes of the slice: x: 4, y: 8, z: 8, core: 2. Of those that a mesh axis runs over, the one named last changes fastest.
Arguments:
- modes_basis: float32 [256, 786432], P('modes', 'rows'), may hold values from -1 to 1
- snapshots: float32 [256, 786432], P('modes', 'rows'), may hold values from -40 to 40
Outputs:
- coefficients: float32 [256, 256], P('modes')
- residual: float32 [256, 786432], P('modes', 'rows')
- gram: float32 [256, 256], P('modes')
- residual_norm: float32 [256], P('modes')
The draws below stay inside these ranges and needn't reach their ends.
All inputs are finite; a program needn't handle non-finite values.
Results may differ from the reference program's by a relative error of at most 0.00027.
Values sent between devices are 32-bit elements; how exact they have to be, the bound alone decides.
A program may use at most 64 MiB of HBM per device.

```python
import math
import jax
import jax.numpy as jnp
from jax import lax

MODES = 256
SNAPS = 256
NDOF = 786432


def basis_draw(key):
    normal_key = jax.random.fold_in(key, 0)
    normal_part = jnp.clip(jax.random.normal(normal_key, (MODES, NDOF), jnp.float32), -6.0, 6.0)
    return normal_part / math.sqrt(NDOF)


def draw_modes_basis(key, part):
    return basis_draw(key).astype(jnp.float32)


def draw_snapshots(key, part):
    basis = basis_draw(key)
    key = jax.random.fold_in(key, 11)
    amp_key, coeff_key, noise_key, row_key, snap_key = jax.random.split(key, 5)
    amplitude = jnp.exp(jax.random.uniform(amp_key, (1, MODES), jnp.float32, 0.0, math.log(30.0)))
    place = jnp.arange(NDOF, dtype=jnp.float32).reshape(1, NDOF) / NDOF
    ramp = jnp.exp(math.log(3.0) * place)
    row_scale = jnp.exp(jax.random.uniform(row_key, (1, NDOF), jnp.float32, math.log(0.2), math.log(2.0)))
    snap_scale = jnp.exp(jax.random.uniform(snap_key, (SNAPS, 1), jnp.float32, math.log(0.3), math.log(3.0)))
    level = 0.04 * math.sqrt(132.0 * MODES / NDOF)
    weights = jnp.clip(jax.random.normal(coeff_key, (SNAPS, MODES), jnp.float32), -4.0, 4.0)
    noise = jnp.clip(jax.random.normal(noise_key, (SNAPS, NDOF), jnp.float32), -6.0, 6.0)
    signal = jnp.dot(amplitude * weights, basis, preferred_element_type=jnp.float32, precision=lax.Precision.HIGHEST)
    return (signal + level * snap_scale * row_scale * ramp * noise).astype(jnp.float32)


def setup_inputs(seed: int = 0) -> dict:
    key_of = jax.random.split(jax.random.key(seed), 3)
    return {
        "modes_basis": draw_modes_basis(jax.random.fold_in(key_of[2], 71), 0),
        "snapshots": draw_snapshots(jax.random.fold_in(key_of[2], 71), 0),
    }


def reference(modes_basis, snapshots):
    coefficients = jnp.dot(snapshots, modes_basis.T, preferred_element_type=jnp.float32, precision=lax.Precision.HIGHEST)
    residual = snapshots - jnp.dot(coefficients, modes_basis, preferred_element_type=jnp.float32, precision=lax.Precision.HIGHEST)
    gram = jnp.dot(residual, residual.T, preferred_element_type=jnp.float32, precision=lax.Precision.HIGHEST) / NDOF
    residual_norm = jnp.sqrt(lax.optimization_barrier(jnp.sum(residual * residual, axis=1)) / NDOF)
    return (coefficients, residual, gram, residual_norm)
```

```python
import functools

import jax
import jax.numpy as jnp
from jax import lax
from jax.experimental import pallas as pl
from jax.experimental.pallas import tpu as pltpu
from jax.sharding import PartitionSpec as P

MESH = pl.DeviceIdType.MESH
NX, NY, NZ = 4, 8, 8
CHUNKS = 3


def product(left, right, contract_right):
    return lax.dot_general(
        left,
        right,
        (((1,), (contract_right,)), ((), ())),
        precision=lax.Precision.HIGHEST,
        preferred_element_type=jnp.float32,
    )


def kernel(
    total_rows,
    phi_ref,
    s_ref,
    coef_ref,
    res_ref,
    gram_ref,
    norm_ref,
    phib,
    sb,
    rb,
    cpart,
    ccore,
    cx,
    cfirst,
    csecond,
    cfull,
    gpart,
    gcore,
    gx,
    gfirst,
    gsecond,
    gpair,
    csum,
    gsum,
    cmid,
    gmid,
    in_send,
    in_recv,
    own_sem,
    c_send,
    c_recv,
    g_send,
    g_recv,
    out_send,
    out_recv,
    out_own,
):
    block, local_cols = phi_ref.shape
    hub_cols = local_cols // NX
    width = hub_cols // CHUNKS
    half = block // 2
    quarter = half // 2

    rows = lax.axis_index("rows")
    x = lax.axis_index("modes")
    core = lax.rem(rows, 2)
    y = lax.rem(lax.div(rows, 2), NY)
    z = lax.div(rows, 2 * NY)

    def x_peer(d):
        return lax.rem(x + d, NX)

    def x_device(d):
        return (rows, x_peer(d))

    def y_device(d):
        return ((z * NY + lax.rem(y + d, NY)) * 2 + core, x)

    def z_device(d):
        return ((lax.rem(z + d, NZ) * NY + y) * 2 + core, x)

    sibling = ((z * NY + y) * 2 + (1 - core), x)

    barrier = pltpu.get_barrier_semaphore()
    for d in range(1, NX):
        pl.semaphore_signal(barrier, inc=1, device_id=x_device(d), device_id_type=MESH)
    for d in range(1, NY):
        pl.semaphore_signal(barrier, inc=1, device_id=y_device(d), device_id_type=MESH)
    for d in range(1, NZ):
        pl.semaphore_signal(barrier, inc=1, device_id=z_device(d), device_id_type=MESH)
    pl.semaphore_signal(barrier, inc=1, device_id=sibling, device_id_type=MESH)
    pl.semaphore_wait(barrier, (NX - 1) + (NY - 1) + (NZ - 1) + 1)

    pending = []

    def send(src, dst, ssem, rsem, device):
        copy = pltpu.make_async_remote_copy(
            src_ref=src, dst_ref=dst, send_sem=ssem, recv_sem=rsem, device_id=device, device_id_type=MESH
        )
        copy.start()
        pending.append(copy)
        return copy

    def block_rows(index):
        return pl.ds(pl.multiple_of(index * block, block), block)

    arrivals, own = [], []
    for k in range(CHUNKS):
        here = pl.ds(k * width, width)
        chunk_copies = []
        for d in (2, 1, 3):
            there = pl.ds(pl.multiple_of(x_peer(d) * hub_cols + k * width, 128), width)
            for i, (src, dst) in enumerate(((phi_ref, phib), (s_ref, sb))):
                chunk_copies.append(
                    send(
                        src.at[:, there],
                        dst.at[block_rows(x), here],
                        in_send.at[k, i, d - 1],
                        in_recv.at[k, i, d - 1],
                        x_device(d),
                    )
                )
        arrivals.append(chunk_copies)
        mine = pl.ds(pl.multiple_of(x * hub_cols + k * width, 128), width)
        own_copies = []
        for i, (src, dst) in enumerate(((phi_ref, phib), (s_ref, sb))):
            copy = pltpu.make_async_copy(src.at[:, mine], dst.at[block_rows(x), here], own_sem.at[k, i])
            copy.start()
            own_copies.append(copy)
        own.append(own_copies)

    acc = None
    for k in range(CHUNKS):
        for copy in own[k]:
            copy.wait()
        for copy in arrivals[k]:
            copy.wait_recv()
        here = pl.ds(k * width, width)
        term = product(sb[:, here], phib[:, here], 1)
        acc = term if acc is None else acc + term
    cpart[...] = acc.reshape(cpart.shape)

    def reduce_grid(part, from_core, from_x, mid, first, second, total, ssem, rsem):
        copy = send(part.at[:, 1 - core], from_core, ssem.at[0], rsem.at[0], sibling)
        copy.wait_recv()
        mid[...] = part[:, core] + from_core[...]
        copies = []
        for d in (2, 1, 3):
            copies.append(send(mid.at[x_peer(d)], from_x.at[x], ssem.at[d], rsem.at[d], x_device(d)))
        from_x[x] = mid[x]
        for copy in copies:
            copy.wait_recv()
        value = (from_x[0] + from_x[1]) + (from_x[2] + from_x[3])
        first[0, y] = value[:quarter]
        first[1, z] = value[quarter:]
        base = NX
        copies = []
        for d in (4, 3, 5, 2, 6, 1, 7):
            copies.append(
                send(first.at[0, y], first.at[0, y], ssem.at[base + d], rsem.at[base + d], y_device(d))
            )
            copies.append(
                send(first.at[1, z], first.at[1, z], ssem.at[base + 8 + d], rsem.at[base + 8 + d], z_device(d))
            )
        for copy in copies:
            copy.wait_recv()
        second[0, z] = jnp.sum(first[0], axis=0)
        second[1, y] = jnp.sum(first[1], axis=0)
        base = NX + 16
        copies = []
        for d in (4, 3, 5, 2, 6, 1, 7):
            copies.append(
                send(second.at[0, z], second.at[0, z], ssem.at[base + d], rsem.at[base + d], z_device(d))
            )
            copies.append(
                send(second.at[1, y], second.at[1, y], ssem.at[base + 8 + d], rsem.at[base + 8 + d], y_device(d))
            )
        for copy in copies:
            copy.wait_recv()
        total[:quarter] = jnp.sum(second[0], axis=0)
        total[quarter:] = jnp.sum(second[1], axis=0)

    reduce_grid(cpart, ccore, cx, cmid, cfirst, csecond, csum, c_send, c_recv)
    base = NX + 32
    copies = []
    for d in (2, 1, 3):
        copies.append(send(csum, cfull.at[core, x], c_send.at[base + d], c_recv.at[base + d], x_device(d)))
    cfull[core, x] = csum[...]
    for copy in copies:
        copy.wait_recv()
    copy = send(cfull.at[core], cfull.at[core], c_send.at[base], c_recv.at[base], sibling)
    copy.wait_recv()
    coef_ref[:half] = cfull[0, x]
    coef_ref[half:] = cfull[1, x]
    coefficients = jnp.concatenate(
        [cfull[c, a] for a in range(NX) for c in range(2)], axis=0
    )

    acc = None
    returns, own = [], []
    for k in range(CHUNKS):
        here = pl.ds(k * width, width)
        residual = sb[:, here] - product(coefficients, phib[:, here], 0)
        rb[:, here] = residual
        mine = pl.ds(pl.multiple_of(x * hub_cols + k * width, 128), width)
        for d in (2, 1, 3):
            returns.append(
                send(
                    rb.at[block_rows(x_peer(d)), here],
                    res_ref.at[:, mine],
                    out_send.at[k, d - 1],
                    out_recv.at[k, d - 1],
                    x_device(d),
                )
            )
        copy = pltpu.make_async_copy(rb.at[block_rows(x), here], res_ref.at[:, mine], out_own.at[k])
        copy.start()
        own.append(copy)
    for k in range(CHUNKS):
        here = pl.ds(k * width, width)
        residual = rb[:, here]
        term = product(residual, residual, 1)
        acc = term if acc is None else acc + term
    gpart[...] = acc.reshape(gpart.shape)

    reduce_grid(gpart, gcore, gx, gmid, gfirst, gsecond, gsum, g_send, g_recv)
    base = NX + 32
    gpair[core] = gsum[...]
    copy = send(gpair.at[core], gpair.at[core], g_send.at[base], g_recv.at[base], sibling)
    copy.wait_recv()
    gram = jnp.concatenate([gpair[0], gpair[1]], axis=0) / total_rows
    gram_ref[...] = gram
    column = lax.broadcasted_iota(jnp.int32, gram.shape, 1)
    row = lax.broadcasted_iota(jnp.int32, gram.shape, 0)
    diagonal = jnp.sum(jnp.where(column == row + x * block, gram, 0.0), axis=0, keepdims=True)
    diagonal = functools.reduce(jnp.add, [diagonal[:, a * block : (a + 1) * block] for a in range(NX)])
    norm_ref[...] = jnp.sqrt(diagonal)

    for copy in returns:
        copy.wait_recv()
    for copy in own:
        copy.wait()
    for copy in pending:
        copy.wait_send()


def per_device(modes_basis, snapshots):
    block, local_cols = modes_basis.shape
    size = block * NX
    hub_cols = local_cols // NX
    half, quarter = block // 2, block // 4
    total_rows = local_cols * lax.axis_size("rows")
    f32 = jnp.float32
    sems = NX + 32 + 4
    hbm = pl.BlockSpec(memory_space=pltpu.HBM)
    vmem = pl.BlockSpec(memory_space=pltpu.VMEM)
    part = pltpu.VMEM((NX, 2, half, size), f32)
    quad = pltpu.VMEM((NX, half, size), f32)
    ring = pltpu.VMEM((2, NY, quarter, size), f32)
    outs = pl.pallas_call(
        functools.partial(kernel, float(total_rows)),
        out_shape=(
            jax.ShapeDtypeStruct((block, size), f32),
            jax.ShapeDtypeStruct((block, local_cols), f32),
            jax.ShapeDtypeStruct((block, size), f32),
            jax.ShapeDtypeStruct((1, block), f32),
        ),
        in_specs=[hbm, hbm],
        out_specs=(vmem, hbm, vmem, vmem),
        scratch_shapes=[
            pltpu.VMEM((size, hub_cols), f32),
            pltpu.VMEM((size, hub_cols), f32),
            pltpu.VMEM((size, hub_cols), f32),
            part,
            quad,
            quad,
            ring,
            ring,
            pltpu.VMEM((2, NX, half, size), f32),
            part,
            quad,
            quad,
            ring,
            ring,
            pltpu.VMEM((2, half, size), f32),
            pltpu.VMEM((half, size), f32),
            pltpu.VMEM((half, size), f32),
            quad,
            quad,
            pltpu.SemaphoreType.DMA((CHUNKS, 2, NX - 1)),
            pltpu.SemaphoreType.DMA((CHUNKS, 2, NX - 1)),
            pltpu.SemaphoreType.DMA((CHUNKS, 2)),
            pltpu.SemaphoreType.DMA((sems,)),
            pltpu.SemaphoreType.DMA((sems,)),
            pltpu.SemaphoreType.DMA((sems,)),
            pltpu.SemaphoreType.DMA((sems,)),
            pltpu.SemaphoreType.DMA((CHUNKS, NX - 1)),
            pltpu.SemaphoreType.DMA((CHUNKS, NX - 1)),
            pltpu.SemaphoreType.DMA((CHUNKS,)),
        ],
        compiler_params=pltpu.CompilerParams(
            collective_id=0, has_side_effects=True, vmem_limit_bytes=56 * 1024 * 1024
        ),
        cost_estimate=pl.CostEstimate(
            flops=6 * size * size * hub_cols, bytes_accessed=12 * block * local_cols, transcendentals=0
        ),
    )(modes_basis, snapshots)
    coefficients, residual, gram, norm = outs
    return coefficients, residual, gram, norm.reshape(block)


def solution(mesh):
    in_specs = (P("modes", "rows"), P("modes", "rows"))
    out_specs = (P("modes", None), P("modes", "rows"), P("modes", None), P("modes"))
    return jax.shard_map(
        per_device, mesh=mesh, in_specs=in_specs, out_specs=out_specs, check_vma=False
    )
```

```python
import functools

import jax
import jax.numpy as jnp
from jax import lax
from jax.experimental import pallas as pl
from jax.experimental.pallas import tpu as pltpu
from jax.sharding import PartitionSpec as P

MESH = pl.DeviceIdType.MESH
NX, NY, NZ = 4, 8, 8
CHUNKS = 3
PIECES = 6
EARLY = 1


def product(left, right, contract_right):
    return lax.dot_general(
        left,
        right,
        (((1,), (contract_right,)), ((), ())),
        precision=lax.Precision.HIGHEST,
        preferred_element_type=jnp.float32,
    )


def plain_product(left, right):
    return lax.dot_general(left, right, (((1,), (1,)), ((), ())), preferred_element_type=jnp.float32)


def kernel(
    total_rows,
    phi_ref,
    s_ref,
    coef_ref,
    res_ref,
    gram_ref,
    norm_ref,
    phib,
    sb,
    rb,
    cpart,
    ccore,
    cx,
    cfirst,
    csecond,
    cfull,
    gpart,
    gcore,
    gx,
    gfirst,
    gsecond,
    gpair,
    csum,
    gsum,
    cmid,
    gmid,
    in_send,
    in_recv,
    own_sem,
    c_send,
    c_recv,
    g_send,
    g_recv,
    out_send,
    out_recv,
    out_own,
):
    block, local_cols = phi_ref.shape
    hub_cols = local_cols // NX
    width = hub_cols // CHUNKS
    half = block // 2
    quarter = half // 2

    rows = lax.axis_index("rows")
    x = lax.axis_index("modes")
    core = lax.rem(rows, 2)
    y = lax.rem(lax.div(rows, 2), NY)
    z = lax.div(rows, 2 * NY)

    def x_peer(d):
        return lax.rem(x + d, NX)

    def x_device(d):
        return (rows, x_peer(d))

    def y_device(d):
        return ((z * NY + lax.rem(y + d, NY)) * 2 + core, x)

    def z_device(d):
        return ((lax.rem(z + d, NZ) * NY + y) * 2 + core, x)

    sibling = ((z * NY + y) * 2 + (1 - core), x)

    barrier = pltpu.get_barrier_semaphore()
    for d in (4, 3, 5, 2, 6, 1, 7):
        pl.semaphore_signal(barrier, inc=1, device_id=y_device(d), device_id_type=MESH)
        pl.semaphore_signal(barrier, inc=1, device_id=z_device(d), device_id_type=MESH)
    for d in (2, 1, 3):
        pl.semaphore_signal(barrier, inc=1, device_id=x_device(d), device_id_type=MESH)
    pl.semaphore_signal(barrier, inc=1, device_id=sibling, device_id_type=MESH)
    pl.semaphore_wait(barrier, (NX - 1) + (NY - 1) + (NZ - 1) + 1)

    pending = []

    def send(src, dst, ssem, rsem, device):
        copy = pltpu.make_async_remote_copy(
            src_ref=src, dst_ref=dst, send_sem=ssem, recv_sem=rsem, device_id=device, device_id_type=MESH
        )
        copy.start()
        pending.append(copy)
        return copy

    def block_rows(index):
        return pl.ds(pl.multiple_of(index * block, block), block)

    arrivals, own = [], []
    for k in range(CHUNKS):
        here = pl.ds(k * width, width)
        chunk_copies = []
        for d in (2, 1, 3):
            there = pl.ds(pl.multiple_of(x_peer(d) * hub_cols + k * width, 128), width)
            for i, (src, dst) in enumerate(((phi_ref, phib), (s_ref, sb))):
                chunk_copies.append(
                    send(
                        src.at[:, there],
                        dst.at[block_rows(x), here],
                        in_send.at[k, i, d - 1],
                        in_recv.at[k, i, d - 1],
                        x_device(d),
                    )
                )
        arrivals.append(chunk_copies)
        mine = pl.ds(pl.multiple_of(x * hub_cols + k * width, 128), width)
        own_copies = []
        for i, (src, dst) in enumerate(((phi_ref, phib), (s_ref, sb))):
            copy = pltpu.make_async_copy(src.at[:, mine], dst.at[block_rows(x), here], own_sem.at[k, i])
            copy.start()
            own_copies.append(copy)
        own.append(own_copies)

    acc = None
    for k in range(CHUNKS):
        for copy in own[k]:
            copy.wait()
        for copy in arrivals[k]:
            copy.wait_recv()
        here = pl.ds(k * width, width)
        term = product(sb[:, here], phib[:, here], 1)
        acc = term if acc is None else acc + term
    cpart[...] = acc.reshape(cpart.shape)

    def reduce_grid(part, from_core, from_x, mid, first, second, total, ssem, rsem, meanwhile):
        copy = send(part.at[:, 1 - core], from_core, ssem.at[0], rsem.at[0], sibling)
        copy.wait_recv()
        mid[...] = part[:, core] + from_core[...]
        copies = []
        for d in (2, 1, 3):
            copies.append(send(mid.at[x_peer(d)], from_x.at[x], ssem.at[d], rsem.at[d], x_device(d)))
        from_x[x] = mid[x]
        for copy in copies:
            copy.wait_recv()
        meanwhile()
        value = (from_x[0] + from_x[1]) + (from_x[2] + from_x[3])
        first[0, y] = value[:quarter]
        first[1, z] = value[quarter:]
        base = NX
        copies = []
        for d in (4, 3, 5, 2, 6, 1, 7):
            copies.append(
                send(first.at[0, y], first.at[0, y], ssem.at[base + d], rsem.at[base + d], y_device(d))
            )
            copies.append(
                send(first.at[1, z], first.at[1, z], ssem.at[base + 8 + d], rsem.at[base + 8 + d], z_device(d))
            )
        for copy in copies:
            copy.wait_recv()
        second[0, z] = jnp.sum(first[0], axis=0)
        second[1, y] = jnp.sum(first[1], axis=0)
        base = NX + 16
        copies = []
        for d in (4, 3, 5, 2, 6, 1, 7):
            copies.append(
                send(second.at[0, z], second.at[0, z], ssem.at[base + d], rsem.at[base + d], z_device(d))
            )
            copies.append(
                send(second.at[1, y], second.at[1, y], ssem.at[base + 8 + d], rsem.at[base + 8 + d], y_device(d))
            )
        for copy in copies:
            copy.wait_recv()
        total[:quarter] = jnp.sum(second[0], axis=0)
        total[quarter:] = jnp.sum(second[1], axis=0)

    reduce_grid(cpart, ccore, cx, cmid, cfirst, csecond, csum, c_send, c_recv, lambda: None)
    base = NX + 32
    cfull[core, x] = csum[...]
    copies = []
    for d in (2, 1, 3):
        copies.append((d, send(csum, cfull.at[core, x], c_send.at[base + d], c_recv.at[base + d], x_device(d))))
    passed = [send(csum, cfull.at[core, x], c_send.at[base], c_recv.at[base], sibling)]
    for d, copy in copies[1:] + copies[:1]:
        copy.wait_recv()
        origin = lax.rem(x + NX - d, NX)
        passed.append(
            send(
                cfull.at[core, origin],
                cfull.at[core, origin],
                c_send.at[base + NX + d],
                c_recv.at[base + NX + d],
                sibling,
            )
        )
    for copy in passed:
        copy.wait_recv()
    coef_ref[:half] = cfull[0, x]
    coef_ref[half:] = cfull[1, x]
    coefficients = jnp.concatenate(
        [cfull[c, a] for a in range(NX) for c in range(2)], axis=0
    )

    returns, own = [], []
    piece = hub_cols // PIECES

    def give_back(index):
        here = pl.ds(index * piece, piece)
        mine = pl.ds(pl.multiple_of(x * hub_cols + index * piece, 128), piece)
        for d in (2, 1, 3):
            returns.append(
                send(
                    rb.at[block_rows(x_peer(d)), here],
                    res_ref.at[:, mine],
                    out_send.at[index, d - 1],
                    out_recv.at[index, d - 1],
                    x_device(d),
                )
            )

    sent = 0
    for k in range(CHUNKS):
        here = pl.ds(k * width, width)
        rb[:, here] = sb[:, here] - product(coefficients, phib[:, here], 0)
        while sent < EARLY and (sent + 1) * piece <= (k + 1) * width:
            give_back(sent)
            sent += 1
    mine = pl.ds(pl.multiple_of(x * hub_cols, 128), hub_cols)
    copy = pltpu.make_async_copy(rb.at[block_rows(x)], res_ref.at[:, mine], out_own)
    copy.start()
    own.append(copy)
    same = cross = None
    for k in range(CHUNKS):
        residual = rb[:, pl.ds(k * width, width)]
        high = residual.astype(jnp.bfloat16)
        low = (residual - high.astype(jnp.float32)).astype(jnp.bfloat16)
        high_high = plain_product(high, high)
        high_low = plain_product(high, low)
        same = high_high if same is None else same + high_high
        cross = high_low if cross is None else cross + high_low
    gpart[...] = (same + (cross + cross.T)).reshape(gpart.shape)

    def send_the_rest():
        for index in range(EARLY, PIECES):
            give_back(index)

    reduce_grid(gpart, gcore, gx, gmid, gfirst, gsecond, gsum, g_send, g_recv, send_the_rest)
    base = NX + 32
    gpair[core] = gsum[...]
    copy = send(gpair.at[core], gpair.at[core], g_send.at[base], g_recv.at[base], sibling)
    copy.wait_recv()
    gram = jnp.concatenate([gpair[0], gpair[1]], axis=0) / total_rows
    gram_ref[...] = gram
    column = lax.broadcasted_iota(jnp.int32, gram.shape, 1)
    row = lax.broadcasted_iota(jnp.int32, gram.shape, 0)
    diagonal = jnp.sum(jnp.where(column == row + x * block, gram, 0.0), axis=0, keepdims=True)
    diagonal = functools.reduce(jnp.add, [diagonal[:, a * block : (a + 1) * block] for a in range(NX)])
    norm_ref[...] = jnp.sqrt(diagonal)

    for copy in returns:
        copy.wait_recv()
    for copy in own:
        copy.wait()
    for copy in pending:
        copy.wait_send()


def copy_kernel(*refs):
    n = (len(refs) - 1) // 2
    sems = refs[-1]
    copies = [pltpu.make_async_copy(refs[i], refs[n + i], sems.at[i]) for i in range(n)]
    for copy in copies:
        copy.start()
    for copy in copies:
        copy.wait()


def copied(arrays):
    hbm = pl.BlockSpec(memory_space=pltpu.HBM)
    return pl.pallas_call(
        copy_kernel,
        out_shape=tuple(jax.ShapeDtypeStruct(a.shape, a.dtype) for a in arrays),
        in_specs=[hbm] * len(arrays),
        out_specs=(hbm,) * len(arrays),
        scratch_shapes=[pltpu.SemaphoreType.DMA((len(arrays),))],
        compiler_params=pltpu.CompilerParams(vmem_limit_bytes=56 * 1024 * 1024),
    )(*arrays)


def per_device(modes_basis, snapshots):
    block, local_cols = modes_basis.shape
    size = block * NX
    hub_cols = local_cols // NX
    half, quarter = block // 2, block // 4
    total_rows = local_cols * lax.axis_size("rows")
    f32 = jnp.float32
    sems = NX + 32 + 2 * NX
    hbm = pl.BlockSpec(memory_space=pltpu.HBM)
    vmem = pl.BlockSpec(memory_space=pltpu.VMEM)
    part = pltpu.VMEM((NX, 2, half, size), f32)
    quad = pltpu.VMEM((NX, half, size), f32)
    ring = pltpu.VMEM((2, NY, quarter, size), f32)
    outs = pl.pallas_call(
        functools.partial(kernel, float(total_rows)),
        out_shape=(
            jax.ShapeDtypeStruct((block, size), f32),
            jax.ShapeDtypeStruct((block, local_cols), f32),
            jax.ShapeDtypeStruct((block, size), f32),
            jax.ShapeDtypeStruct((1, block), f32),
        ),
        in_specs=[hbm, hbm],
        out_specs=(vmem, hbm, vmem, vmem),
        scratch_shapes=[
            pltpu.VMEM((size, hub_cols), f32),
            pltpu.VMEM((size, hub_cols), f32),
            pltpu.VMEM((size, hub_cols), f32),
            part,
            quad,
            quad,
            ring,
            ring,
            pltpu.VMEM((2, NX, half, size), f32),
            part,
            quad,
            quad,
            ring,
            ring,
            pltpu.VMEM((2, half, size), f32),
            pltpu.VMEM((half, size), f32),
            pltpu.VMEM((half, size), f32),
            quad,
            quad,
            pltpu.SemaphoreType.DMA((CHUNKS, 2, NX - 1)),
            pltpu.SemaphoreType.DMA((CHUNKS, 2, NX - 1)),
            pltpu.SemaphoreType.DMA((CHUNKS, 2)),
            pltpu.SemaphoreType.DMA((sems,)),
            pltpu.SemaphoreType.DMA((sems,)),
            pltpu.SemaphoreType.DMA((sems,)),
            pltpu.SemaphoreType.DMA((sems,)),
            pltpu.SemaphoreType.DMA((PIECES, NX - 1)),
            pltpu.SemaphoreType.DMA((PIECES, NX - 1)),
            pltpu.SemaphoreType.DMA,
        ],
        compiler_params=pltpu.CompilerParams(
            collective_id=0, has_side_effects=True, vmem_limit_bytes=56 * 1024 * 1024
        ),
        cost_estimate=pl.CostEstimate(
            flops=6 * size * size * hub_cols, bytes_accessed=12 * block * local_cols, transcendentals=0
        ),
    )(modes_basis, snapshots)
    coefficients, residual, gram, norm = copied(outs)
    return coefficients, residual, gram, norm.reshape(block)


def solution(mesh):
    in_specs = (P("modes", "rows"), P("modes", "rows"))
    out_specs = (P("modes", None), P("modes", "rows"), P("modes", None), P("modes"))
    return jax.shard_map(
        per_device, mesh=mesh, in_specs=in_specs, out_specs=out_specs, check_vma=False
    )
```

```python
import functools

import jax
import jax.numpy as jnp
from jax import lax
from jax.experimental import pallas as pl
from jax.experimental.pallas import tpu as pltpu
from jax.sharding import PartitionSpec as P

MESH = pl.DeviceIdType.MESH
NX, NY, NZ = 4, 8, 8
CHUNKS = 3
PIECES = 6
EARLY = 1


def product(left, right, contract_right):
    return lax.dot_general(
        left,
        right,
        (((1,), (contract_right,)), ((), ())),
        precision=lax.Precision.HIGHEST,
        preferred_element_type=jnp.float32,
    )


def plain_product(left, right):
    return lax.dot_general(left, right, (((1,), (1,)), ((), ())), preferred_element_type=jnp.float32)


def kernel(
    total_rows,
    phi_ref,
    s_ref,
    coef_ref,
    res_ref,
    gram_ref,
    norm_ref,
    phib,
    sb,
    rb,
    cpart,
    ccore,
    cx,
    cfirst,
    csecond,
    cfull,
    gpart,
    gcore,
    gx,
    gfirst,
    gsecond,
    gpair,
    csum,
    gsum,
    cmid,
    gmid,
    in_send,
    in_recv,
    own_sem,
    c_send,
    c_recv,
    g_send,
    g_recv,
    out_send,
    out_recv,
    out_own,
):
    block, local_cols = phi_ref.shape
    hub_cols = local_cols // NX
    width = hub_cols // CHUNKS
    half = block // 2
    quarter = half // 2

    rows = lax.axis_index("rows")
    x = lax.axis_index("modes")
    core = lax.rem(rows, 2)
    y = lax.rem(lax.div(rows, 2), NY)
    z = lax.div(rows, 2 * NY)

    def x_peer(d):
        return lax.rem(x + d, NX)

    def x_device(d):
        return (rows, x_peer(d))

    def y_device(d):
        return ((z * NY + lax.rem(y + d, NY)) * 2 + core, x)

    def z_device(d):
        return ((lax.rem(z + d, NZ) * NY + y) * 2 + core, x)

    sibling = ((z * NY + y) * 2 + (1 - core), x)

    barrier = pltpu.get_barrier_semaphore()
    for d in (4, 3, 5, 2, 6, 1, 7):
        pl.semaphore_signal(barrier, inc=1, device_id=y_device(d), device_id_type=MESH)
        pl.semaphore_signal(barrier, inc=1, device_id=z_device(d), device_id_type=MESH)
    for d in (2, 1, 3):
        pl.semaphore_signal(barrier, inc=1, device_id=x_device(d), device_id_type=MESH)
    pl.semaphore_signal(barrier, inc=1, device_id=sibling, device_id_type=MESH)
    pl.semaphore_wait(barrier, (NX - 1) + (NY - 1) + (NZ - 1) + 1)

    pending = []

    def send(src, dst, ssem, rsem, device):
        copy = pltpu.make_async_remote_copy(
            src_ref=src, dst_ref=dst, send_sem=ssem, recv_sem=rsem, device_id=device, device_id_type=MESH
        )
        copy.start()
        pending.append(copy)
        return copy

    def block_rows(index):
        return pl.ds(pl.multiple_of(index * block, block), block)

    arrivals, own = [], []
    for k in range(CHUNKS):
        here = pl.ds(k * width, width)
        chunk_copies = []
        for d in (2, 1, 3):
            there = pl.ds(pl.multiple_of(x_peer(d) * hub_cols + k * width, 128), width)
            for i, (src, dst) in enumerate(((phi_ref, phib), (s_ref, sb))):
                chunk_copies.append(
                    send(
                        src.at[:, there],
                        dst.at[block_rows(x), here],
                        in_send.at[k, i, d - 1],
                        in_recv.at[k, i, d - 1],
                        x_device(d),
                    )
                )
        arrivals.append(chunk_copies)
        mine = pl.ds(pl.multiple_of(x * hub_cols + k * width, 128), width)
        own_copies = []
        for i, (src, dst) in enumerate(((phi_ref, phib), (s_ref, sb))):
            copy = pltpu.make_async_copy(src.at[:, mine], dst.at[block_rows(x), here], own_sem.at[k, i])
            copy.start()
            own_copies.append(copy)
        own.append(own_copies)

    acc = None
    for k in range(CHUNKS):
        for copy in own[k]:
            copy.wait()
        for copy in arrivals[k]:
            copy.wait_recv()
        here = pl.ds(k * width, width)
        term = product(sb[:, here], phib[:, here], 1)
        acc = term if acc is None else acc + term
    cpart[...] = acc.reshape(cpart.shape)

    def reduce_grid(part, from_core, from_x, mid, first, second, total, ssem, rsem, meanwhile):
        copy = send(part.at[:, 1 - core], from_core, ssem.at[0], rsem.at[0], sibling)
        copy.wait_recv()
        mid[...] = part[:, core] + from_core[...]
        copies = []
        for d in (2, 1, 3):
            copies.append(send(mid.at[x_peer(d)], from_x.at[x], ssem.at[d], rsem.at[d], x_device(d)))
        from_x[x] = mid[x]
        for copy in copies:
            copy.wait_recv()
        meanwhile()
        value = (from_x[0] + from_x[1]) + (from_x[2] + from_x[3])
        first[0, y] = value[:quarter]
        first[1, z] = value[quarter:]
        base = NX
        copies = []
        for d in (4, 3, 5, 2, 6, 1, 7):
            copies.append(
                send(first.at[0, y], first.at[0, y], ssem.at[base + d], rsem.at[base + d], y_device(d))
            )
            copies.append(
                send(first.at[1, z], first.at[1, z], ssem.at[base + 8 + d], rsem.at[base + 8 + d], z_device(d))
            )
        for copy in copies:
            copy.wait_recv()
        second[0, z] = jnp.sum(first[0], axis=0)
        second[1, y] = jnp.sum(first[1], axis=0)
        base = NX + 16
        copies = []
        for d in (4, 3, 5, 2, 6, 1, 7):
            copies.append(
                send(second.at[0, z], second.at[0, z], ssem.at[base + d], rsem.at[base + d], z_device(d))
            )
            copies.append(
                send(second.at[1, y], second.at[1, y], ssem.at[base + 8 + d], rsem.at[base + 8 + d], y_device(d))
            )
        for copy in copies:
            copy.wait_recv()
        total[:quarter] = jnp.sum(second[0], axis=0)
        total[quarter:] = jnp.sum(second[1], axis=0)

    reduce_grid(cpart, ccore, cx, cmid, cfirst, csecond, csum, c_send, c_recv, lambda: None)
    base = NX + 32
    cfull[core, x] = csum[...]
    copies = []
    for d in (2, 1, 3):
        copies.append((d, send(csum, cfull.at[core, x], c_send.at[base + d], c_recv.at[base + d], x_device(d))))
    passed = [send(csum, cfull.at[core, x], c_send.at[base], c_recv.at[base], sibling)]
    for d, copy in copies[1:] + copies[:1]:
        copy.wait_recv()
        origin = lax.rem(x + NX - d, NX)
        passed.append(
            send(
                cfull.at[core, origin],
                cfull.at[core, origin],
                c_send.at[base + NX + d],
                c_recv.at[base + NX + d],
                sibling,
            )
        )
    for copy in passed:
        copy.wait_recv()
    coef_ref[:half] = cfull[0, x]
    coef_ref[half:] = cfull[1, x]
    coefficients = jnp.concatenate(
        [cfull[c, a] for a in range(NX) for c in range(2)], axis=0
    )

    returns, own = [], []
    piece = hub_cols // PIECES

    def give_back(index):
        here = pl.ds(index * piece, piece)
        mine = pl.ds(pl.multiple_of(x * hub_cols + index * piece, 128), piece)
        for d in (2, 1, 3):
            returns.append(
                send(
                    rb.at[block_rows(x_peer(d)), here],
                    res_ref.at[:, mine],
                    out_send.at[index, d - 1],
                    out_recv.at[index, d - 1],
                    x_device(d),
                )
            )

    sent = 0
    for k in range(CHUNKS):
        here = pl.ds(k * width, width)
        rb[:, here] = sb[:, here] - product(coefficients, phib[:, here], 0)
        while sent < EARLY and (sent + 1) * piece <= (k + 1) * width:
            give_back(sent)
            sent += 1
    mine = pl.ds(pl.multiple_of(x * hub_cols, 128), hub_cols)
    copy = pltpu.make_async_copy(rb.at[block_rows(x)], res_ref.at[:, mine], out_own)
    copy.start()
    own.append(copy)
    same = cross = None
    for k in range(CHUNKS):
        residual = rb[:, pl.ds(k * width, width)]
        high = residual.astype(jnp.bfloat16)
        low = (residual - high.astype(jnp.float32)).astype(jnp.bfloat16)
        high_high = plain_product(high, high)
        high_low = plain_product(high, low)
        same = high_high if same is None else same + high_high
        cross = high_low if cross is None else cross + high_low
    gpart[...] = (same + (cross + cross.T)).reshape(gpart.shape)

    def send_the_rest():
        for index in range(EARLY, PIECES):
            give_back(index)

    reduce_grid(gpart, gcore, gx, gmid, gfirst, gsecond, gsum, g_send, g_recv, send_the_rest)
    base = NX + 32
    gpair[core] = gsum[...]
    copy = send(gpair.at[core], gpair.at[core], g_send.at[base], g_recv.at[base], sibling)
    copy.wait_recv()
    gram = jnp.concatenate([gpair[0], gpair[1]], axis=0) / total_rows
    gram_ref[...] = gram
    column = lax.broadcasted_iota(jnp.int32, gram.shape, 1)
    row = lax.broadcasted_iota(jnp.int32, gram.shape, 0)
    diagonal = jnp.sum(jnp.where(column == row + x * block, gram, 0.0), axis=0, keepdims=True)
    diagonal = functools.reduce(jnp.add, [diagonal[:, a * block : (a + 1) * block] for a in range(NX)])
    norm_ref[...] = jnp.sqrt(diagonal)

    for copy in returns:
        copy.wait_recv()
    for copy in own:
        copy.wait()
    for copy in pending:
        copy.wait_send()


def copy_kernel(*refs):
    n = (len(refs) - 1) // 2
    sems = refs[-1]
    copies = [pltpu.make_async_copy(refs[i], refs[n + i], sems.at[i]) for i in range(n)]
    for copy in copies:
        copy.start()
    for copy in copies:
        copy.wait()


def copied(arrays):
    hbm = pl.BlockSpec(memory_space=pltpu.HBM)
    vmem = pl.BlockSpec(memory_space=pltpu.VMEM)
    return pl.pallas_call(
        copy_kernel,
        out_shape=tuple(jax.ShapeDtypeStruct(a.shape, a.dtype) for a in arrays),
        in_specs=[vmem] * len(arrays),
        out_specs=(hbm,) * len(arrays),
        scratch_shapes=[pltpu.SemaphoreType.DMA((len(arrays),))],
    )(*arrays)


def per_device(modes_basis, snapshots):
    block, local_cols = modes_basis.shape
    size = block * NX
    hub_cols = local_cols // NX
    half, quarter = block // 2, block // 4
    total_rows = local_cols * lax.axis_size("rows")
    f32 = jnp.float32
    sems = NX + 32 + 2 * NX
    hbm = pl.BlockSpec(memory_space=pltpu.HBM)
    vmem = pl.BlockSpec(memory_space=pltpu.VMEM)
    part = pltpu.VMEM((NX, 2, half, size), f32)
    quad = pltpu.VMEM((NX, half, size), f32)
    ring = pltpu.VMEM((2, NY, quarter, size), f32)
    outs = pl.pallas_call(
        functools.partial(kernel, float(total_rows)),
        out_shape=(
            pltpu.VMEM((block, size), f32),
            pltpu.VMEM((block, local_cols), f32),
            pltpu.VMEM((block, size), f32),
            pltpu.VMEM((1, block), f32),
        ),
        in_specs=[hbm, hbm],
        out_specs=(vmem, vmem, vmem, vmem),
        scratch_shapes=[
            pltpu.VMEM((size, hub_cols), f32),
            pltpu.VMEM((size, hub_cols), f32),
            pltpu.VMEM((size, hub_cols), f32),
            part,
            quad,
            quad,
            ring,
            ring,
            pltpu.VMEM((2, NX, half, size), f32),
            part,
            quad,
            quad,
            ring,
            ring,
            pltpu.VMEM((2, half, size), f32),
            pltpu.VMEM((half, size), f32),
            pltpu.VMEM((half, size), f32),
            quad,
            quad,
            pltpu.SemaphoreType.DMA((CHUNKS, 2, NX - 1)),
            pltpu.SemaphoreType.DMA((CHUNKS, 2, NX - 1)),
            pltpu.SemaphoreType.DMA((CHUNKS, 2)),
            pltpu.SemaphoreType.DMA((sems,)),
            pltpu.SemaphoreType.DMA((sems,)),
            pltpu.SemaphoreType.DMA((sems,)),
            pltpu.SemaphoreType.DMA((sems,)),
            pltpu.SemaphoreType.DMA((PIECES, NX - 1)),
            pltpu.SemaphoreType.DMA((PIECES, NX - 1)),
            pltpu.SemaphoreType.DMA,
        ],
        compiler_params=pltpu.CompilerParams(
            collective_id=0, has_side_effects=True, vmem_limit_bytes=56 * 1024 * 1024
        ),
        cost_estimate=pl.CostEstimate(
            flops=6 * size * size * hub_cols, bytes_accessed=12 * block * local_cols, transcendentals=0
        ),
    )(modes_basis, snapshots)
    coefficients, residual, gram, norm = copied(outs)
    return coefficients, residual, gram, norm.reshape(block)


def solution(mesh):
    in_specs = (P("modes", "rows"), P("modes", "rows"))
    out_specs = (P("modes", None), P("modes", "rows"), P("modes", None), P("modes"))
    return jax.shard_map(
        per_device, mesh=mesh, in_specs=in_specs, out_specs=out_specs, check_vma=False
    )
```

```python
import functools

import jax
import jax.numpy as jnp
from jax import lax
from jax.experimental import pallas as pl
from jax.experimental.pallas import tpu as pltpu
from jax.sharding import PartitionSpec as P

MESH = pl.DeviceIdType.MESH
NX, NY, NZ = 4, 8, 8
CHUNKS = 3
PIECES = 6
EARLY = 1
MIDDLE = 2


def product(left, right, contract_right):
    return lax.dot_general(
        left,
        right,
        (((1,), (contract_right,)), ((), ())),
        precision=lax.Precision.HIGHEST,
        preferred_element_type=jnp.float32,
    )


def plain_product(left, right):
    return lax.dot_general(left, right, (((1,), (1,)), ((), ())), preferred_element_type=jnp.float32)


def kernel(
    total_rows,
    phi_ref,
    s_ref,
    coef_ref,
    res_ref,
    gram_ref,
    norm_ref,
    phib,
    sb,
    rb,
    cpart,
    ccore,
    cx,
    cfirst,
    csecond,
    cfull,
    gpart,
    gcore,
    gx,
    gfirst,
    gsecond,
    gpair,
    csum,
    gsum,
    cmid,
    gmid,
    in_send,
    in_recv,
    own_sem,
    c_send,
    c_recv,
    g_send,
    g_recv,
    out_send,
    out_recv,
    out_own,
):
    block, local_cols = phi_ref.shape
    hub_cols = local_cols // NX
    width = hub_cols // CHUNKS
    half = block // 2
    quarter = half // 2

    rows = lax.axis_index("rows")
    x = lax.axis_index("modes")
    core = lax.rem(rows, 2)
    y = lax.rem(lax.div(rows, 2), NY)
    z = lax.div(rows, 2 * NY)

    def x_peer(d):
        return lax.rem(x + d, NX)

    def x_device(d):
        return (rows, x_peer(d))

    def y_device(d):
        return ((z * NY + lax.rem(y + d, NY)) * 2 + core, x)

    def z_device(d):
        return ((lax.rem(z + d, NZ) * NY + y) * 2 + core, x)

    sibling = ((z * NY + y) * 2 + (1 - core), x)

    barrier = pltpu.get_barrier_semaphore()
    for d in (4, 3, 5, 2, 6, 1, 7):
        pl.semaphore_signal(barrier, inc=1, device_id=y_device(d), device_id_type=MESH)
        pl.semaphore_signal(barrier, inc=1, device_id=z_device(d), device_id_type=MESH)
    for d in (2, 1, 3):
        pl.semaphore_signal(barrier, inc=1, device_id=x_device(d), device_id_type=MESH)
    pl.semaphore_signal(barrier, inc=1, device_id=sibling, device_id_type=MESH)
    pl.semaphore_wait(barrier, (NX - 1) + (NY - 1) + (NZ - 1) + 1)

    pending = []

    def send(src, dst, ssem, rsem, device):
        copy = pltpu.make_async_remote_copy(
            src_ref=src, dst_ref=dst, send_sem=ssem, recv_sem=rsem, device_id=device, device_id_type=MESH
        )
        copy.start()
        pending.append(copy)
        return copy

    def block_rows(index):
        return pl.ds(pl.multiple_of(index * block, block), block)

    arrivals, own = [], []
    for k in range(CHUNKS):
        here = pl.ds(k * width, width)
        chunk_copies = []
        for d in (2, 1, 3):
            there = pl.ds(pl.multiple_of(x_peer(d) * hub_cols + k * width, 128), width)
            for i, (src, dst) in enumerate(((phi_ref, phib), (s_ref, sb))):
                chunk_copies.append(
                    send(
                        src.at[:, there],
                        dst.at[block_rows(x), here],
                        in_send.at[k, i, d - 1],
                        in_recv.at[k, i, d - 1],
                        x_device(d),
                    )
                )
        arrivals.append(chunk_copies)
        mine = pl.ds(pl.multiple_of(x * hub_cols + k * width, 128), width)
        own_copies = []
        for i, (src, dst) in enumerate(((phi_ref, phib), (s_ref, sb))):
            copy = pltpu.make_async_copy(src.at[:, mine], dst.at[block_rows(x), here], own_sem.at[k, i])
            copy.start()
            own_copies.append(copy)
        own.append(own_copies)

    acc = None
    for k in range(CHUNKS):
        for copy in own[k]:
            copy.wait()
        for copy in arrivals[k]:
            copy.wait_recv()
        here = pl.ds(k * width, width)
        term = product(sb[:, here], phib[:, here], 1)
        acc = term if acc is None else acc + term
    cpart[...] = acc.reshape(cpart.shape)

    def reduce_grid(part, from_core, from_x, mid, first, second, total, ssem, rsem, meanwhile):
        copy = send(part.at[:, 1 - core], from_core, ssem.at[0], rsem.at[0], sibling)
        copy.wait_recv()
        mid[...] = part[:, core] + from_core[...]
        copies = []
        for d in (2, 1, 3):
            copies.append(send(mid.at[x_peer(d)], from_x.at[x], ssem.at[d], rsem.at[d], x_device(d)))
        from_x[x] = mid[x]
        meanwhile[0]()
        for copy in copies:
            copy.wait_recv()
        meanwhile[1]()
        value = (from_x[0] + from_x[1]) + (from_x[2] + from_x[3])
        first[0, y] = value[:quarter]
        first[1, z] = value[quarter:]
        base = NX
        copies = []
        for d in (4, 3, 5, 2, 6, 1, 7):
            copies.append(
                send(first.at[0, y], first.at[0, y], ssem.at[base + d], rsem.at[base + d], y_device(d))
            )
            copies.append(
                send(first.at[1, z], first.at[1, z], ssem.at[base + 8 + d], rsem.at[base + 8 + d], z_device(d))
            )
        for copy in copies:
            copy.wait_recv()
        second[0, z] = jnp.sum(first[0], axis=0)
        second[1, y] = jnp.sum(first[1], axis=0)
        base = NX + 16
        copies = []
        for d in (4, 3, 5, 2, 6, 1, 7):
            copies.append(
                send(second.at[0, z], second.at[0, z], ssem.at[base + d], rsem.at[base + d], z_device(d))
            )
            copies.append(
                send(second.at[1, y], second.at[1, y], ssem.at[base + 8 + d], rsem.at[base + 8 + d], y_device(d))
            )
        for copy in copies:
            copy.wait_recv()
        total[:quarter] = jnp.sum(second[0], axis=0)
        total[quarter:] = jnp.sum(second[1], axis=0)

    reduce_grid(cpart, ccore, cx, cmid, cfirst, csecond, csum, c_send, c_recv, (lambda: None, lambda: None))
    base = NX + 32
    cfull[core, x] = csum[...]
    copies = []
    for d in (2, 1, 3):
        copies.append((d, send(csum, cfull.at[core, x], c_send.at[base + d], c_recv.at[base + d], x_device(d))))
    passed = [send(csum, cfull.at[core, x], c_send.at[base], c_recv.at[base], sibling)]
    for d, copy in copies[1:] + copies[:1]:
        copy.wait_recv()
        origin = lax.rem(x + NX - d, NX)
        passed.append(
            send(
                cfull.at[core, origin],
                cfull.at[core, origin],
                c_send.at[base + NX + d],
                c_recv.at[base + NX + d],
                sibling,
            )
        )
    for copy in passed:
        copy.wait_recv()
    coef_ref[:half] = cfull[0, x]
    coef_ref[half:] = cfull[1, x]
    coefficients = jnp.concatenate(
        [cfull[c, a] for a in range(NX) for c in range(2)], axis=0
    )

    returns, own = [], []
    piece = hub_cols // PIECES

    def give_back(index):
        here = pl.ds(index * piece, piece)
        mine = pl.ds(pl.multiple_of(x * hub_cols + index * piece, 128), piece)
        for d in (2, 1, 3):
            returns.append(
                send(
                    rb.at[block_rows(x_peer(d)), here],
                    res_ref.at[:, mine],
                    out_send.at[index, d - 1],
                    out_recv.at[index, d - 1],
                    x_device(d),
                )
            )

    sent = 0
    for k in range(CHUNKS):
        here = pl.ds(k * width, width)
        rb[:, here] = sb[:, here] - product(coefficients, phib[:, here], 0)
        while sent < EARLY and (sent + 1) * piece <= (k + 1) * width:
            give_back(sent)
            sent += 1
    mine = pl.ds(pl.multiple_of(x * hub_cols, 128), hub_cols)
    copy = pltpu.make_async_copy(rb.at[block_rows(x)], res_ref.at[:, mine], out_own)
    copy.start()
    own.append(copy)
    same = cross = None
    for k in range(CHUNKS):
        residual = rb[:, pl.ds(k * width, width)]
        high = residual.astype(jnp.bfloat16)
        low = (residual - high.astype(jnp.float32)).astype(jnp.bfloat16)
        high_high = plain_product(high, high)
        high_low = plain_product(high, low)
        same = high_high if same is None else same + high_high
        cross = high_low if cross is None else cross + high_low
    gpart[...] = (same + (cross + cross.T)).reshape(gpart.shape)

    def send_some():
        for index in range(EARLY, MIDDLE):
            give_back(index)

    def send_the_rest():
        for index in range(MIDDLE, PIECES):
            give_back(index)

    reduce_grid(
        gpart, gcore, gx, gmid, gfirst, gsecond, gsum, g_send, g_recv, (send_some, send_the_rest)
    )
    base = NX + 32
    gpair[core] = gsum[...]
    copy = send(gpair.at[core], gpair.at[core], g_send.at[base], g_recv.at[base], sibling)
    copy.wait_recv()
    gram = jnp.concatenate([gpair[0], gpair[1]], axis=0) / total_rows
    gram_ref[...] = gram
    column = lax.broadcasted_iota(jnp.int32, gram.shape, 1)
    row = lax.broadcasted_iota(jnp.int32, gram.shape, 0)
    diagonal = jnp.sum(jnp.where(column == row + x * block, gram, 0.0), axis=0, keepdims=True)
    diagonal = functools.reduce(jnp.add, [diagonal[:, a * block : (a + 1) * block] for a in range(NX)])
    norm_ref[...] = jnp.sqrt(diagonal)

    for copy in returns:
        copy.wait_recv()
    for copy in own:
        copy.wait()
    for copy in pending:
        copy.wait_send()


def copy_kernel(*refs):
    n = (len(refs) - 1) // 2
    sems = refs[-1]
    copies = [pltpu.make_async_copy(refs[i], refs[n + i], sems.at[i]) for i in range(n)]
    for copy in copies:
        copy.start()
    for copy in copies:
        copy.wait()


def copied(arrays):
    hbm = pl.BlockSpec(memory_space=pltpu.HBM)
    vmem = pl.BlockSpec(memory_space=pltpu.VMEM)
    return pl.pallas_call(
        copy_kernel,
        out_shape=tuple(jax.ShapeDtypeStruct(a.shape, a.dtype) for a in arrays),
        in_specs=[vmem] * len(arrays),
        out_specs=(hbm,) * len(arrays),
        scratch_shapes=[pltpu.SemaphoreType.DMA((len(arrays),))],
        compiler_params=pltpu.CompilerParams(vmem_limit_bytes=1024 * 1024),
    )(*arrays)


def per_device(modes_basis, snapshots):
    block, local_cols = modes_basis.shape
    size = block * NX
    hub_cols = local_cols // NX
    half, quarter = block // 2, block // 4
    total_rows = local_cols * lax.axis_size("rows")
    f32 = jnp.float32
    sems = NX + 32 + 2 * NX
    hbm = pl.BlockSpec(memory_space=pltpu.HBM)
    vmem = pl.BlockSpec(memory_space=pltpu.VMEM)
    part = pltpu.VMEM((NX, 2, half, size), f32)
    quad = pltpu.VMEM((NX, half, size), f32)
    ring = pltpu.VMEM((2, NY, quarter, size), f32)
    outs = pl.pallas_call(
        functools.partial(kernel, float(total_rows)),
        out_shape=(
            pltpu.VMEM((block, size), f32),
            pltpu.VMEM((block, local_cols), f32),
            pltpu.VMEM((block, size), f32),
            pltpu.VMEM((1, block), f32),
        ),
        in_specs=[hbm, hbm],
        out_specs=(vmem, vmem, vmem, vmem),
        scratch_shapes=[
            pltpu.VMEM((size, hub_cols), f32),
            pltpu.VMEM((size, hub_cols), f32),
            pltpu.VMEM((size, hub_cols), f32),
            part,
            quad,
            quad,
            ring,
            ring,
            pltpu.VMEM((2, NX, half, size), f32),
            part,
            quad,
            quad,
            ring,
            ring,
            pltpu.VMEM((2, half, size), f32),
            pltpu.VMEM((half, size), f32),
            pltpu.VMEM((half, size), f32),
            quad,
            quad,
            pltpu.SemaphoreType.DMA((CHUNKS, 2, NX - 1)),
            pltpu.SemaphoreType.DMA((CHUNKS, 2, NX - 1)),
            pltpu.SemaphoreType.DMA((CHUNKS, 2)),
            pltpu.SemaphoreType.DMA((sems,)),
            pltpu.SemaphoreType.DMA((sems,)),
            pltpu.SemaphoreType.DMA((sems,)),
            pltpu.SemaphoreType.DMA((sems,)),
            pltpu.SemaphoreType.DMA((PIECES, NX - 1)),
            pltpu.SemaphoreType.DMA((PIECES, NX - 1)),
            pltpu.SemaphoreType.DMA,
        ],
        compiler_params=pltpu.CompilerParams(
            collective_id=0, has_side_effects=True, vmem_limit_bytes=56 * 1024 * 1024
        ),
        cost_estimate=pl.CostEstimate(
            flops=6 * size * size * hub_cols, bytes_accessed=12 * block * local_cols, transcendentals=0
        ),
    )(modes_basis, snapshots)
    coefficients, residual, gram, norm = copied(outs)
    return coefficients, residual, gram, norm.reshape(block)


def solution(mesh):
    in_specs = (P("modes", "rows"), P("modes", "rows"))
    out_specs = (P("modes", None), P("modes", "rows"), P("modes", None), P("modes"))
    return jax.shard_map(
        per_device, mesh=mesh, in_specs=in_specs, out_specs=out_specs, check_vma=False
    )
```

```python
import functools

import jax
import jax.numpy as jnp
from jax import lax
from jax.experimental import pallas as pl
from jax.experimental.pallas import tpu as pltpu
from jax.sharding import PartitionSpec as P

MESH = pl.DeviceIdType.MESH
NX, NY, NZ = 4, 8, 8
CHUNKS = 6
WINDOW = 4
PARTS = 3
PIECES = 6
EARLY = 1
MIDDLE = 1


def product(left, right, contract_right):
    return lax.dot_general(
        left,
        right,
        (((1,), (contract_right,)), ((), ())),
        precision=lax.Precision.HIGHEST,
        preferred_element_type=jnp.float32,
    )


def plain_product(left, right):
    return lax.dot_general(left, right, (((1,), (1,)), ((), ())), preferred_element_type=jnp.float32)


def kernel(
    total_rows,
    phi_ref,
    s_ref,
    coef_ref,
    res_ref,
    gram_ref,
    norm_ref,
    phib,
    sb,
    rb,
    cpart,
    ccore,
    cx,
    cfirst,
    csecond,
    cfull,
    gpart,
    gcore,
    gx,
    gfirst,
    gsecond,
    gpair,
    csum,
    gsum,
    cmid,
    gmid,
    in_send,
    in_recv,
    own_sem,
    c_send,
    c_recv,
    g_send,
    g_recv,
    out_send,
    out_recv,
    out_own,
    phi_last,
    s_last,
    last_send,
    last_recv,
    last_own,
):
    block, local_cols = phi_ref.shape
    hub_cols = local_cols // NX
    width = hub_cols // CHUNKS
    half = block // 2
    quarter = half // 2

    rows = lax.axis_index("rows")
    x = lax.axis_index("modes")
    core = lax.rem(rows, 2)
    y = lax.rem(lax.div(rows, 2), NY)
    z = lax.div(rows, 2 * NY)

    def x_peer(d):
        return lax.rem(x + d, NX)

    def x_device(d):
        return (rows, x_peer(d))

    def y_device(d):
        return ((z * NY + lax.rem(y + d, NY)) * 2 + core, x)

    def z_device(d):
        return ((lax.rem(z + d, NZ) * NY + y) * 2 + core, x)

    sibling = ((z * NY + y) * 2 + (1 - core), x)

    barrier = pltpu.get_barrier_semaphore()
    for d in (4, 3, 5, 2, 6, 1, 7):
        pl.semaphore_signal(barrier, inc=1, device_id=y_device(d), device_id_type=MESH)
        pl.semaphore_signal(barrier, inc=1, device_id=z_device(d), device_id_type=MESH)
    for d in (2, 1, 3):
        pl.semaphore_signal(barrier, inc=1, device_id=x_device(d), device_id_type=MESH)
    pl.semaphore_signal(barrier, inc=1, device_id=sibling, device_id_type=MESH)
    pl.semaphore_wait(barrier, (NX - 1) + (NY - 1) + (NZ - 1) + 1)

    pending = []

    def send(src, dst, ssem, rsem, device):
        copy = pltpu.make_async_remote_copy(
            src_ref=src, dst_ref=dst, send_sem=ssem, recv_sem=rsem, device_id=device, device_id_type=MESH
        )
        copy.start()
        pending.append(copy)
        return copy

    def settle(keep):
        done = pending[: len(pending) - keep]
        del pending[: len(done)]
        for copy in done:
            copy.wait_send()

    def block_rows(index):
        return pl.ds(pl.multiple_of(index * block, block), block)

    arrivals, own = [], []

    def fetch(k):
        here = pl.ds(k * width, width)
        chunk_copies = []
        for d in (2, 1, 3):
            there = pl.ds(pl.multiple_of(x_peer(d) * hub_cols + k * width, 128), width)
            for i, (src, dst) in enumerate(((phi_ref, phib), (s_ref, sb))):
                chunk_copies.append(
                    send(
                        src.at[:, there],
                        dst.at[block_rows(x), here],
                        in_send.at[k, i, d - 1],
                        in_recv.at[k, i, d - 1],
                        x_device(d),
                    )
                )
        arrivals.append(chunk_copies)
        mine = pl.ds(pl.multiple_of(x * hub_cols + k * width, 128), width)
        own_copies = []
        for i, (src, dst) in enumerate(((phi_ref, phib), (s_ref, sb))):
            copy = pltpu.make_async_copy(src.at[:, mine], dst.at[block_rows(x), here], own_sem.at[k, i])
            copy.start()
            own_copies.append(copy)
        own.append(own_copies)

    for k in range(WINDOW):
        fetch(k)

    acc = None
    for k in range(CHUNKS):
        for copy in own[k]:
            copy.wait()
        for copy in arrivals[k]:
            copy.wait_recv()
        if k + WINDOW < CHUNKS:
            fetch(k + WINDOW)
        here = pl.ds(k * width, width)
        term = product(sb[:, here], phib[:, here], 1)
        acc = term if acc is None else acc + term
    cpart[...] = acc.reshape(cpart.shape)

    def reduce_grid(part, from_core, from_x, mid, first, second, total, ssem, rsem, meanwhile):
        copy = send(part.at[:, 1 - core], from_core, ssem.at[0], rsem.at[0], sibling)
        copy.wait_recv()
        mid[...] = part[:, core] + from_core[...]
        copies = []
        for d in (2, 1, 3):
            copies.append(send(mid.at[x_peer(d)], from_x.at[x], ssem.at[d], rsem.at[d], x_device(d)))
        from_x[x] = mid[x]
        meanwhile[0]()
        for copy in copies:
            copy.wait_recv()
        meanwhile[1]()
        value = (from_x[0] + from_x[1]) + (from_x[2] + from_x[3])
        first[0, y] = value[:quarter]
        first[1, z] = value[quarter:]
        base = NX
        copies = []
        for d in (4, 3, 5, 2, 6, 1, 7):
            copies.append(
                send(first.at[0, y], first.at[0, y], ssem.at[base + d], rsem.at[base + d], y_device(d))
            )
            copies.append(
                send(first.at[1, z], first.at[1, z], ssem.at[base + 8 + d], rsem.at[base + 8 + d], z_device(d))
            )
        meanwhile[2]()
        for copy in copies:
            copy.wait_recv()
        second[0, z] = jnp.sum(first[0], axis=0)
        second[1, y] = jnp.sum(first[1], axis=0)
        base = NX + 16
        copies = []
        for d in (4, 3, 5, 2, 6, 1, 7):
            copies.append(
                send(second.at[0, z], second.at[0, z], ssem.at[base + d], rsem.at[base + d], z_device(d))
            )
            copies.append(
                send(second.at[1, y], second.at[1, y], ssem.at[base + 8 + d], rsem.at[base + 8 + d], y_device(d))
            )
        meanwhile[3]()
        for copy in copies:
            copy.wait_recv()
        total[:quarter] = jnp.sum(second[0], axis=0)
        total[quarter:] = jnp.sum(second[1], axis=0)

    piece = hub_cols // PIECES
    last = (PIECES - 1) * piece
    extra = []

    def nothing():
        pass

    def gather_last():
        for e in (2, 1, 3):
            for d in range(1, NX):
                owner = lax.rem(x + e + d, NX)
                there = pl.ds(pl.multiple_of(owner * hub_cols + last, 128), piece)
                extra.append(
                    send(
                        phi_ref.at[:, there],
                        phi_last.at[d - 1, block_rows(x)],
                        last_send.at[e - 1, d - 1],
                        last_recv.at[e - 1, d - 1],
                        x_device(e),
                    )
                )

    extra_own = []
    for d in range(1, NX):
        there = pl.ds(pl.multiple_of(x_peer(d) * hub_cols + last, 128), piece)
        pairs = ((phi_ref.at[:, there], phi_last.at[d - 1, block_rows(x)]), (s_ref.at[:, there], s_last.at[d - 1]))
        for i, (src, dst) in enumerate(pairs):
            copy = pltpu.make_async_copy(src, dst, last_own.at[i, d - 1])
            copy.start()
            extra_own.append(copy)

    reduce_grid(
        cpart,
        ccore,
        cx,
        cmid,
        cfirst,
        csecond,
        csum,
        c_send,
        c_recv,
        (nothing, gather_last, lambda: settle((NY - 1) + (NZ - 1) + (NX - 1) ** 2), nothing),
    )
    base = NX + 32
    cfull[core, x] = csum[...]
    copies = []
    for d in (2, 1, 3):
        copies.append((d, send(csum, cfull.at[core, x], c_send.at[base + d], c_recv.at[base + d], x_device(d))))
    passed = [send(csum, cfull.at[core, x], c_send.at[base], c_recv.at[base], sibling)]
    for d, copy in copies[1:] + copies[:1]:
        copy.wait_recv()
        origin = lax.rem(x + NX - d, NX)
        passed.append(
            send(
                cfull.at[core, origin],
                cfull.at[core, origin],
                c_send.at[base + NX + d],
                c_recv.at[base + NX + d],
                sibling,
            )
        )
    for copy in passed:
        copy.wait_recv()
    coef_ref[:half] = cfull[0, x]
    coef_ref[half:] = cfull[1, x]
    coefficients = jnp.concatenate(
        [cfull[c, a] for a in range(NX) for c in range(2)], axis=0
    )

    returns, own = [], []

    def give_back(index):
        here = pl.ds(index * piece, piece)
        mine = pl.ds(pl.multiple_of(x * hub_cols + index * piece, 128), piece)
        for d in (2, 1, 3):
            returns.append(
                send(
                    rb.at[block_rows(x_peer(d)), here],
                    res_ref.at[:, mine],
                    out_send.at[index, d - 1],
                    out_recv.at[index, d - 1],
                    x_device(d),
                )
            )

    sent = 0
    same = cross = None
    width = hub_cols // PARTS
    for k in range(PARTS):
        here = pl.ds(k * width, width)
        residual = sb[:, here] - product(coefficients, phib[:, here], 0)
        rb[:, here] = residual
        while sent < EARLY and (sent + 1) * piece <= (k + 1) * width:
            give_back(sent)
            sent += 1
        high = residual.astype(jnp.bfloat16)
        low = (residual - high.astype(jnp.float32)).astype(jnp.bfloat16)
        high_high = plain_product(high, high)
        high_low = plain_product(high, low)
        same = high_high if same is None else same + high_high
        cross = high_low if cross is None else cross + high_low
    gpart[...] = (same + (cross + cross.T)).reshape(gpart.shape)

    def send_some():
        for index in range(EARLY, MIDDLE):
            give_back(index)

    def send_the_rest():
        mine = pl.ds(pl.multiple_of(x * hub_cols, 128), hub_cols)
        copy = pltpu.make_async_copy(rb.at[block_rows(x)], res_ref.at[:, mine], out_own)
        copy.start()
        own.append(copy)
        for index in range(MIDDLE, PIECES - 1):
            give_back(index)

    def own_residual():
        for copy in extra_own:
            copy.wait()
        for copy in extra:
            copy.wait_recv()
        mine = jnp.concatenate([cfull[0, x], cfull[1, x]], axis=0)
        for d in range(1, NX):
            there = pl.ds(pl.multiple_of(x_peer(d) * hub_cols + last, 128), piece)
            res_ref[:, there] = s_last[d - 1] - product(mine, phi_last[d - 1], 0)

    later = (NX - 1) * (PIECES - 1) + (NY - 1) + (NZ - 1)

    reduce_grid(
        gpart,
        gcore,
        gx,
        gmid,
        gfirst,
        gsecond,
        gsum,
        g_send,
        g_recv,
        (send_some, send_the_rest, own_residual, lambda: settle(later + (NY - 1) + (NZ - 1))),
    )
    base = NX + 32
    gpair[core] = gsum[...]
    copy = send(gpair.at[core], gpair.at[core], g_send.at[base], g_recv.at[base], sibling)
    copy.wait_recv()
    gram = jnp.concatenate([gpair[0], gpair[1]], axis=0) / total_rows
    gram_ref[...] = gram
    column = lax.broadcasted_iota(jnp.int32, gram.shape, 1)
    row = lax.broadcasted_iota(jnp.int32, gram.shape, 0)
    diagonal = jnp.sum(jnp.where(column == row + x * block, gram, 0.0), axis=0, keepdims=True)
    diagonal = functools.reduce(jnp.add, [diagonal[:, a * block : (a + 1) * block] for a in range(NX)])
    norm_ref[...] = jnp.sqrt(diagonal)

    for copy in returns:
        copy.wait_recv()
    for copy in own:
        copy.wait()
    settle(0)


def copy_kernel(*refs):
    n = (len(refs) - 1) // 2
    sems = refs[-1]
    copies = [pltpu.make_async_copy(refs[i], refs[n + i], sems.at[i]) for i in range(n)]
    for copy in copies:
        copy.start()
    for copy in copies:
        copy.wait()


def copied(arrays):
    hbm = pl.BlockSpec(memory_space=pltpu.HBM)
    vmem = pl.BlockSpec(memory_space=pltpu.VMEM)
    return pl.pallas_call(
        copy_kernel,
        out_shape=tuple(jax.ShapeDtypeStruct(a.shape, a.dtype) for a in arrays),
        in_specs=[vmem] * len(arrays),
        out_specs=(hbm,) * len(arrays),
        scratch_shapes=[pltpu.SemaphoreType.DMA((len(arrays),))],
        compiler_params=pltpu.CompilerParams(vmem_limit_bytes=1024 * 1024),
    )(*arrays)


def per_device(modes_basis, snapshots):
    block, local_cols = modes_basis.shape
    size = block * NX
    hub_cols = local_cols // NX
    half, quarter = block // 2, block // 4
    total_rows = local_cols * lax.axis_size("rows")
    f32 = jnp.float32
    sems = NX + 32 + 2 * NX
    hbm = pl.BlockSpec(memory_space=pltpu.HBM)
    vmem = pl.BlockSpec(memory_space=pltpu.VMEM)
    part = pltpu.VMEM((NX, 2, half, size), f32)
    quad = pltpu.VMEM((NX, half, size), f32)
    ring = pltpu.VMEM((2, NY, quarter, size), f32)
    outs = pl.pallas_call(
        functools.partial(kernel, float(total_rows)),
        out_shape=(
            pltpu.VMEM((block, size), f32),
            pltpu.VMEM((block, local_cols), f32),
            pltpu.VMEM((block, size), f32),
            pltpu.VMEM((1, block), f32),
        ),
        in_specs=[hbm, hbm],
        out_specs=(vmem, vmem, vmem, vmem),
        scratch_shapes=[
            pltpu.VMEM((size, hub_cols), f32),
            pltpu.VMEM((size, hub_cols), f32),
            pltpu.VMEM((size, hub_cols), f32),
            part,
            quad,
            quad,
            ring,
            ring,
            pltpu.VMEM((2, NX, half, size), f32),
            part,
            quad,
            quad,
            ring,
            ring,
            pltpu.VMEM((2, half, size), f32),
            pltpu.VMEM((half, size), f32),
            pltpu.VMEM((half, size), f32),
            quad,
            quad,
            pltpu.SemaphoreType.DMA((CHUNKS, 2, NX - 1)),
            pltpu.SemaphoreType.DMA((CHUNKS, 2, NX - 1)),
            pltpu.SemaphoreType.DMA((CHUNKS, 2)),
            pltpu.SemaphoreType.DMA((sems,)),
            pltpu.SemaphoreType.DMA((sems,)),
            pltpu.SemaphoreType.DMA((sems,)),
            pltpu.SemaphoreType.DMA((sems,)),
            pltpu.SemaphoreType.DMA((PIECES, NX - 1)),
            pltpu.SemaphoreType.DMA((PIECES, NX - 1)),
            pltpu.SemaphoreType.DMA,
            pltpu.VMEM((NX - 1, size, hub_cols // PIECES), f32),
            pltpu.VMEM((NX - 1, block, hub_cols // PIECES), f32),
            pltpu.SemaphoreType.DMA((NX - 1, NX - 1)),
            pltpu.SemaphoreType.DMA((NX - 1, NX - 1)),
            pltpu.SemaphoreType.DMA((2, NX - 1)),
        ],
        compiler_params=pltpu.CompilerParams(
            collective_id=0, has_side_effects=True, vmem_limit_bytes=56 * 1024 * 1024
        ),
        cost_estimate=pl.CostEstimate(
            flops=6 * size * size * hub_cols, bytes_accessed=12 * block * local_cols, transcendentals=0
        ),
    )(modes_basis, snapshots)
    coefficients, residual, gram, norm = copied(outs)
    return coefficients, residual, gram, norm.reshape(block)


def solution(mesh):
    in_specs = (P("modes", "rows"), P("modes", "rows"))
    out_specs = (P("modes", None), P("modes", "rows"), P("modes", None), P("modes"))
    return jax.shard_map(
        per_device, mesh=mesh, in_specs=in_specs, out_specs=out_specs, check_vma=False
    )
```

```python
import functools

import jax
import jax.numpy as jnp
from jax import lax
from jax.experimental import pallas as pl
from jax.experimental.pallas import tpu as pltpu
from jax.sharding import PartitionSpec as P

MESH = pl.DeviceIdType.MESH
NX, NY, NZ = 4, 8, 8
CHUNKS = 6
WINDOW = 4
PARTS = 3
PIECES = 6
EARLY = 1
MIDDLE = 1


def product(left, right, contract_right):
    return lax.dot_general(
        left,
        right,
        (((1,), (contract_right,)), ((), ())),
        precision=lax.Precision.HIGHEST,
        preferred_element_type=jnp.float32,
    )


def plain_product(left, right):
    return lax.dot_general(left, right, (((1,), (1,)), ((), ())), preferred_element_type=jnp.float32)


def kernel(
    total_rows,
    phi_ref,
    s_ref,
    coef_ref,
    res_ref,
    gram_ref,
    norm_ref,
    phib,
    sb,
    rb,
    cpart,
    ccore,
    cx,
    cfirst_y,
    cfirst_z,
    csecond_y,
    csecond_z,
    cfull,
    gpart,
    gcore,
    gx,
    gfirst_y,
    gfirst_z,
    gsecond_y,
    gsecond_z,
    gpair,
    csum,
    gsum,
    cmid,
    gmid,
    in_send,
    in_recv,
    own_sem,
    c_send,
    c_recv,
    g_send,
    g_recv,
    out_send,
    out_recv,
    out_own,
    phi_last,
    s_last,
    last_send,
    last_recv,
    last_own,
):
    block, local_cols = phi_ref.shape
    hub_cols = local_cols // NX
    width = hub_cols // CHUNKS
    half = block // 2
    quarter = half // 4

    rows = lax.axis_index("rows")
    x = lax.axis_index("modes")
    core = lax.rem(rows, 2)
    y = lax.rem(lax.div(rows, 2), NY)
    z = lax.div(rows, 2 * NY)

    def x_peer(d):
        return lax.rem(x + d, NX)

    def x_device(d):
        return (rows, x_peer(d))

    def y_device(d):
        return ((z * NY + lax.rem(y + d, NY)) * 2 + core, x)

    def z_device(d):
        return ((lax.rem(z + d, NZ) * NY + y) * 2 + core, x)

    sibling = ((z * NY + y) * 2 + (1 - core), x)
    side = lax.rem(y, 2)
    pair = lax.div(y, 2)
    beside = y + 1 - 2 * side

    def near(d, e, f=0):
        row = beside if e else y
        return ((z * NY + row) * 2 + (1 - core if f else core), x_peer(d))

    group = [(d, e) for d in (2, 1, 3, 0) for e in (1, 0) if d or e]

    barrier = pltpu.get_barrier_semaphore()
    y_devices = [y_device(d) for d in (4, 2, 6)]
    z_devices = [z_device(d) for d in (4, 3, 5, 2, 6, 1, 7)]
    partners = [near(d, e) for d, e in group] + y_devices + z_devices + [sibling, near(0, 1, 1)]
    for partner in partners:
        pl.semaphore_signal(barrier, inc=1, device_id=partner, device_id_type=MESH)
    pl.semaphore_wait(barrier, len(partners))

    pending = []

    def send(src, dst, ssem, rsem, device):
        copy = pltpu.make_async_remote_copy(
            src_ref=src, dst_ref=dst, send_sem=ssem, recv_sem=rsem, device_id=device, device_id_type=MESH
        )
        copy.start()
        pending.append(copy)
        return copy

    def settle(keep):
        done = pending[: len(pending) - keep]
        del pending[: len(done)]
        for copy in done:
            copy.wait_send()

    def block_rows(index):
        return pl.ds(pl.multiple_of(index * block, block), block)

    arrivals, own = [], []

    def fetch(k):
        here = pl.ds(k * width, width)
        chunk_copies = []
        for d in (2, 1, 3):
            there = pl.ds(pl.multiple_of(x_peer(d) * hub_cols + k * width, 128), width)
            for i, (src, dst) in enumerate(((phi_ref, phib), (s_ref, sb))):
                chunk_copies.append(
                    send(
                        src.at[:, there],
                        dst.at[block_rows(x), here],
                        in_send.at[k, i, d - 1],
                        in_recv.at[k, i, d - 1],
                        x_device(d),
                    )
                )
        arrivals.append(chunk_copies)
        mine = pl.ds(pl.multiple_of(x * hub_cols + k * width, 128), width)
        own_copies = []
        for i, (src, dst) in enumerate(((phi_ref, phib), (s_ref, sb))):
            copy = pltpu.make_async_copy(src.at[:, mine], dst.at[block_rows(x), here], own_sem.at[k, i])
            copy.start()
            own_copies.append(copy)
        own.append(own_copies)

    for k in range(WINDOW):
        fetch(k)

    piece = hub_cols // PIECES
    last = (PIECES - 1) * piece
    extra_own = []
    for d in range(1, NX):
        there = pl.ds(pl.multiple_of(x_peer(d) * hub_cols + last, 128), piece)
        pairs = ((phi_ref.at[:, there], phi_last.at[d - 1, block_rows(x)]), (s_ref.at[:, there], s_last.at[d - 1]))
        for i, (src, dst) in enumerate(pairs):
            copy = pltpu.make_async_copy(src, dst, last_own.at[i, d - 1])
            copy.start()
            extra_own.append(copy)

    acc = None
    for k in range(CHUNKS):
        for copy in own[k]:
            copy.wait()
        for copy in arrivals[k]:
            copy.wait_recv()
        if k + WINDOW < CHUNKS:
            fetch(k + WINDOW)
        here = pl.ds(k * width, width)
        term = product(sb[:, here], phib[:, here], 1)
        acc = term if acc is None else acc + term
    cpart[...] = acc.reshape(cpart.shape)

    class Ring:
        def __init__(self, slots, mine, devices, ssem, rsem):
            for device in devices:
                pltpu.make_async_remote_copy(
                    src_ref=slots.at[mine],
                    dst_ref=slots.at[mine],
                    send_sem=ssem,
                    recv_sem=rsem,
                    device_id=device,
                    device_id_type=MESH,
                ).start()
            self.all = pltpu.make_async_remote_copy(
                src_ref=slots.at[pl.ds(0, len(devices))],
                dst_ref=slots.at[pl.ds(0, len(devices))],
                send_sem=ssem,
                recv_sem=rsem,
                device_id=devices[0],
                device_id_type=MESH,
            )
            self.wait_recv = self.all.wait_recv
            self.wait_send = self.all.wait_send

    def ring(slots, mine, devices, ssem, rsem):
        copies = Ring(slots, mine, devices, ssem, rsem)
        pending.append(copies)
        return copies

    def reduce_grid(part, from_core, from_near, mid, first, second, total, ssem, rsem, meanwhile):
        copy = send(part.at[:, 1 - core], from_core, ssem.at[0], rsem.at[0], sibling)
        copy.wait_recv()
        mid[...] = part[:, core] + from_core[...]
        copies = []
        for k, (d, e) in enumerate(group):
            to_side = 1 - side if e else side
            copies.append(
                send(mid.at[x_peer(d), to_side], from_near.at[x, side], ssem.at[k + 1], rsem.at[k + 1], near(d, e))
            )
        from_near[x, side] = mid[x, side]
        meanwhile[0]()
        for copy in copies:
            copy.wait_recv()
        value = jnp.sum(from_near[...].reshape((2 * NX,) + total.shape), axis=0)
        along_y, along_z = first
        along_y[pair] = value[:quarter]
        along_z[z] = value[quarter:]
        copies = [
            ring(along_y, pair, y_devices, ssem.at[8], rsem.at[8]),
            ring(along_z, z, z_devices, ssem.at[9], rsem.at[9]),
        ]
        meanwhile[1]()
        meanwhile[2]()
        for copy in copies:
            copy.wait_recv()
        then_z, then_y = second
        then_z[z] = jnp.sum(along_y[...], axis=0)
        then_y[pair] = jnp.sum(along_z[...], axis=0)
        copies = [
            ring(then_z, z, z_devices, ssem.at[10], rsem.at[10]),
            ring(then_y, pair, y_devices, ssem.at[11], rsem.at[11]),
        ]
        meanwhile[3]()
        for copy in copies:
            copy.wait_recv()
        total[:quarter] = jnp.sum(then_z[...], axis=0)
        total[quarter:] = jnp.sum(then_y[...], axis=0)

    extra = []

    def nothing():
        pass

    def gather_last():
        for e in (2, 1, 3):
            for d in range(1, NX):
                owner = lax.rem(x + e + d, NX)
                there = pl.ds(pl.multiple_of(owner * hub_cols + last, 128), piece)
                extra.append(
                    send(
                        phi_ref.at[:, there],
                        phi_last.at[d - 1, block_rows(x)],
                        last_send.at[e - 1, d - 1],
                        last_recv.at[e - 1, d - 1],
                        x_device(e),
                    )
                )

    reduce_grid(
        cpart,
        ccore,
        cx,
        cmid,
        (cfirst_y, cfirst_z),
        (csecond_z, csecond_y),
        csum,
        c_send,
        c_recv,
        (nothing, gather_last, lambda: settle(2 + (NX - 1) ** 2), nothing),
    )
    cfull[core, x, side] = csum[...]
    copies = []
    for k, (d, e) in enumerate(group):
        copies.append(
            send(csum, cfull.at[core, x, side], c_send.at[12 + k], c_recv.at[12 + k], near(d, e))
        )
    for copy in copies:
        copy.wait_recv()
    copy = send(cfull.at[core], cfull.at[core], c_send.at[20], c_recv.at[20], sibling)
    copy.wait_recv()

    def rows_of(a):
        return [cfull[c, a].reshape(half, NX * block) for c in range(2)]

    coefficients = jnp.concatenate(
        [part for a in range(NX) for part in rows_of(a)], axis=0
    )

    returns, own = [], []

    def give_back(index):
        here = pl.ds(index * piece, piece)
        mine = pl.ds(pl.multiple_of(x * hub_cols + index * piece, 128), piece)
        for d in (2, 1, 3):
            returns.append(
                send(
                    rb.at[block_rows(x_peer(d)), here],
                    res_ref.at[:, mine],
                    out_send.at[index, d - 1],
                    out_recv.at[index, d - 1],
                    x_device(d),
                )
            )

    sent = 0
    same = cross = None
    width = hub_cols // PARTS
    for k in range(PARTS):
        here = pl.ds(k * width, width)
        residual = sb[:, here] - product(coefficients, phib[:, here], 0)
        rb[:, here] = residual
        while sent < EARLY and (sent + 1) * piece <= (k + 1) * width:
            give_back(sent)
            sent += 1
        high = residual.astype(jnp.bfloat16)
        low = (residual - high.astype(jnp.float32)).astype(jnp.bfloat16)
        high_high = plain_product(high, high)
        high_low = plain_product(high, low)
        same = high_high if same is None else same + high_high
        cross = high_low if cross is None else cross + high_low
    gpart[...] = (same + (cross + cross.T)).reshape(gpart.shape)

    def send_some():
        for index in range(EARLY, MIDDLE):
            give_back(index)

    def send_the_rest():
        mine = pl.ds(pl.multiple_of(x * hub_cols, 128), hub_cols)
        copy = pltpu.make_async_copy(rb.at[block_rows(x)], res_ref.at[:, mine], out_own)
        copy.start()
        own.append(copy)
        for index in range(MIDDLE, PIECES - 1):
            give_back(index)

    def own_residual():
        for copy in extra_own:
            copy.wait()
        for copy in extra:
            copy.wait_recv()
        mine = jnp.concatenate(rows_of(x), axis=0)
        coef_ref[...] = mine
        for d in range(1, NX):
            there = pl.ds(pl.multiple_of(x_peer(d) * hub_cols + last, 128), piece)
            res_ref[:, there] = s_last[d - 1] - product(mine, phi_last[d - 1], 0)

    later = (NX - 1) * (PIECES - 1) + 2

    reduce_grid(
        gpart,
        gcore,
        gx,
        gmid,
        (gfirst_y, gfirst_z),
        (gsecond_z, gsecond_y),
        gsum,
        g_send,
        g_recv,
        (send_some, send_the_rest, own_residual, lambda: settle(later + 2)),
    )
    gpair[core, side] = gsum[...]
    copies = []
    for k, partner in enumerate((near(0, 1, 1), near(0, 1), sibling)):
        copies.append(send(gpair.at[core, side], gpair.at[core, side], g_send.at[12 + k], g_recv.at[12 + k], partner))
    for done in returns:
        done.wait_recv()
    for done in own:
        done.wait()
    settle(3)
    for copy in copies:
        copy.wait_recv()
    gram = gpair[...].reshape(block, NX * block) / total_rows
    gram_ref[...] = gram
    column = lax.broadcasted_iota(jnp.int32, gram.shape, 1)
    row = lax.broadcasted_iota(jnp.int32, gram.shape, 0)
    diagonal = jnp.sum(jnp.where(column == row + x * block, gram, 0.0), axis=0, keepdims=True)
    diagonal = functools.reduce(jnp.add, [diagonal[:, a * block : (a + 1) * block] for a in range(NX)])
    norm_ref[...] = jnp.sqrt(diagonal)

    settle(0)


def copy_kernel(*refs):
    n = (len(refs) - 1) // 2
    sems = refs[-1]
    copies = [pltpu.make_async_copy(refs[i], refs[n + i], sems.at[i]) for i in range(n)]
    for copy in copies:
        copy.start()
    for copy in copies:
        copy.wait()


def copied(arrays):
    hbm = pl.BlockSpec(memory_space=pltpu.HBM)
    vmem = pl.BlockSpec(memory_space=pltpu.VMEM)
    return pl.pallas_call(
        copy_kernel,
        out_shape=tuple(jax.ShapeDtypeStruct(a.shape, a.dtype) for a in arrays),
        in_specs=[vmem] * len(arrays),
        out_specs=(hbm,) * len(arrays),
        scratch_shapes=[pltpu.SemaphoreType.DMA((len(arrays),))],
        compiler_params=pltpu.CompilerParams(vmem_limit_bytes=1024 * 1024),
    )(*arrays)


def per_device(modes_basis, snapshots):
    block, local_cols = modes_basis.shape
    size = block * NX
    hub_cols = local_cols // NX
    share = block // 4
    total_rows = local_cols * lax.axis_size("rows")
    f32 = jnp.float32
    sems = 24
    hbm = pl.BlockSpec(memory_space=pltpu.HBM)
    vmem = pl.BlockSpec(memory_space=pltpu.VMEM)
    part = pltpu.VMEM((NX, 2, 2, share, size), f32)
    near = pltpu.VMEM((NX, 2, share, size), f32)
    rings = [pltpu.VMEM((n, share // 2, size), f32) for n in (NY // 2, NZ, NY // 2, NZ)]
    own = pltpu.VMEM((share, size), f32)
    outs = pl.pallas_call(
        functools.partial(kernel, float(total_rows)),
        out_shape=(
            pltpu.VMEM((block, size), f32),
            pltpu.VMEM((block, local_cols), f32),
            pltpu.VMEM((block, size), f32),
            pltpu.VMEM((1, block), f32),
        ),
        in_specs=[hbm, hbm],
        out_specs=(vmem, vmem, vmem, vmem),
        scratch_shapes=[
            pltpu.VMEM((size, hub_cols), f32),
            pltpu.VMEM((size, hub_cols), f32),
            pltpu.VMEM((size, hub_cols), f32),
            part,
            near,
            near,
            *rings,
            pltpu.VMEM((2, NX, 2, share, size), f32),
            part,
            near,
            near,
            *rings,
            pltpu.VMEM((2, 2, share, size), f32),
            own,
            own,
            near,
            near,
            pltpu.SemaphoreType.DMA((CHUNKS, 2, NX - 1)),
            pltpu.SemaphoreType.DMA((CHUNKS, 2, NX - 1)),
            pltpu.SemaphoreType.DMA((CHUNKS, 2)),
            pltpu.SemaphoreType.DMA((sems,)),
            pltpu.SemaphoreType.DMA((sems,)),
            pltpu.SemaphoreType.DMA((sems,)),
            pltpu.SemaphoreType.DMA((sems,)),
            pltpu.SemaphoreType.DMA((PIECES, NX - 1)),
            pltpu.SemaphoreType.DMA((PIECES, NX - 1)),
            pltpu.SemaphoreType.DMA,
            pltpu.VMEM((NX - 1, size, hub_cols // PIECES), f32),
            pltpu.VMEM((NX - 1, block, hub_cols // PIECES), f32),
            pltpu.SemaphoreType.DMA((NX - 1, NX - 1)),
            pltpu.SemaphoreType.DMA((NX - 1, NX - 1)),
            pltpu.SemaphoreType.DMA((2, NX - 1)),
        ],
        compiler_params=pltpu.CompilerParams(
            collective_id=0, has_side_effects=True, vmem_limit_bytes=56 * 1024 * 1024
        ),
        cost_estimate=pl.CostEstimate(
            flops=6 * size * size * hub_cols, bytes_accessed=12 * block * local_cols, transcendentals=0
        ),
    )(modes_basis, snapshots)
    coefficients, residual, gram, norm = copied(outs)
    return coefficients, residual, gram, norm.reshape(block)


def solution(mesh):
    in_specs = (P("modes", "rows"), P("modes", "rows"))
    out_specs = (P("modes", None), P("modes", "rows"), P("modes", None), P("modes"))
    return jax.shard_map(
        per_device, mesh=mesh, in_specs=in_specs, out_specs=out_specs, check_vma=False
    )
```

```python
import functools

import jax
import jax.numpy as jnp
from jax import lax
from jax.experimental import pallas as pl
from jax.experimental.pallas import tpu as pltpu
from jax.sharding import PartitionSpec as P

MESH = pl.DeviceIdType.MESH
NX, NY, NZ = 4, 8, 8
CHUNKS = 6
WINDOW = 4
PARTS = 3
PIECES = 6
EARLY = 1
MIDDLE = 1


def product(left, right, contract_right):
    return lax.dot_general(
        left,
        right,
        (((1,), (contract_right,)), ((), ())),
        precision=lax.Precision.HIGHEST,
        preferred_element_type=jnp.float32,
    )


def plain_product(left, right):
    return lax.dot_general(left, right, (((1,), (1,)), ((), ())), preferred_element_type=jnp.float32)


def kernel(
    total_rows,
    phi_ref,
    s_ref,
    coef_ref,
    res_ref,
    gram_ref,
    norm_ref,
    phib,
    sb,
    rb,
    cpart,
    ccore,
    cx,
    cfirst_y,
    cfirst_z,
    csecond_y,
    csecond_z,
    cfull,
    gpart,
    gcore,
    gx,
    gfirst_y,
    gfirst_z,
    gsecond_y,
    gsecond_z,
    gpair,
    csum,
    gsum,
    cmid,
    gmid,
    in_send,
    in_recv,
    own_sem,
    c_send,
    c_recv,
    g_send,
    g_recv,
    out_send,
    out_recv,
    out_own,
    phi_last,
    s_last,
    last_send,
    last_recv,
    last_own,
):
    block, local_cols = phi_ref.shape
    hub_cols = local_cols // NX
    width = hub_cols // CHUNKS
    half = block // 2
    quarter = half // 4

    rows = lax.axis_index("rows")
    x = lax.axis_index("modes")
    core = lax.rem(rows, 2)
    y = lax.rem(lax.div(rows, 2), NY)
    z = lax.div(rows, 2 * NY)

    def x_peer(d):
        return lax.rem(x + d, NX)

    def x_device(d):
        return (rows, x_peer(d))

    def y_device(d):
        return ((z * NY + lax.rem(y + d, NY)) * 2 + core, x)

    def z_device(d):
        return ((lax.rem(z + d, NZ) * NY + y) * 2 + core, x)

    sibling = ((z * NY + y) * 2 + (1 - core), x)
    side = lax.rem(y, 2)
    pair = lax.div(y, 2)
    beside = y + 1 - 2 * side

    def near(d, e, f=0):
        row = beside if e else y
        return ((z * NY + row) * 2 + (1 - core if f else core), x_peer(d))

    group = [(d, e) for d in (2, 1, 3, 0) for e in (1, 0) if d or e]

    barrier = pltpu.get_barrier_semaphore()
    y_devices = [y_device(d) for d in (4, 2, 6)]
    z_devices = [z_device(d) for d in (4, 3, 5, 2, 6, 1, 7)]
    partners = [near(d, e) for d, e in group] + y_devices + z_devices + [sibling, near(0, 1, 1)]
    for partner in partners:
        pl.semaphore_signal(barrier, inc=1, device_id=partner, device_id_type=MESH)
    pl.semaphore_wait(barrier, len(partners))

    pending = []

    def send(src, dst, ssem, rsem, device):
        copy = pltpu.make_async_remote_copy(
            src_ref=src, dst_ref=dst, send_sem=ssem, recv_sem=rsem, device_id=device, device_id_type=MESH
        )
        copy.start()
        pending.append(copy)
        return copy

    def settle(keep):
        done = pending[: len(pending) - keep]
        del pending[: len(done)]
        for copy in done:
            copy.wait_send()

    def block_rows(index):
        return pl.ds(pl.multiple_of(index * block, block), block)

    arrivals, own = [], []

    def fetch(k):
        here = pl.ds(k * width, width)
        chunk_copies = []
        for d in (2, 1, 3):
            there = pl.ds(pl.multiple_of(x_peer(d) * hub_cols + k * width, 128), width)
            for i, (src, dst) in enumerate(((phi_ref, phib), (s_ref, sb))):
                chunk_copies.append(
                    send(
                        src.at[:, there],
                        dst.at[block_rows(x), here],
                        in_send.at[k, i, d - 1],
                        in_recv.at[k, i, d - 1],
                        x_device(d),
                    )
                )
        arrivals.append(chunk_copies)
        mine = pl.ds(pl.multiple_of(x * hub_cols + k * width, 128), width)
        own_copies = []
        for i, (src, dst) in enumerate(((phi_ref, phib), (s_ref, sb))):
            copy = pltpu.make_async_copy(src.at[:, mine], dst.at[block_rows(x), here], own_sem.at[k, i])
            copy.start()
            own_copies.append(copy)
        own.append(own_copies)

    for k in range(WINDOW):
        fetch(k)

    piece = hub_cols // PIECES
    last = (PIECES - 1) * piece
    extra_own = []
    for d in range(1, NX):
        there = pl.ds(pl.multiple_of(x_peer(d) * hub_cols + last, 128), piece)
        pairs = ((phi_ref.at[:, there], phi_last.at[d - 1, block_rows(x)]), (s_ref.at[:, there], s_last.at[d - 1]))
        for i, (src, dst) in enumerate(pairs):
            copy = pltpu.make_async_copy(src, dst, last_own.at[i, d - 1])
            copy.start()
            extra_own.append(copy)

    acc = None
    for k in range(CHUNKS):
        for copy in own[k]:
            copy.wait()
        for copy in arrivals[k]:
            copy.wait_recv()
        if k + WINDOW < CHUNKS:
            fetch(k + WINDOW)
        here = pl.ds(k * width, width)
        term = product(sb[:, here], phib[:, here], 1)
        acc = term if acc is None else acc + term
    cpart[...] = acc.reshape(cpart.shape)

    class Ring:
        def __init__(self, slots, mine, devices, ssem, rsem):
            for device in devices:
                pltpu.make_async_remote_copy(
                    src_ref=slots.at[mine],
                    dst_ref=slots.at[mine],
                    send_sem=ssem,
                    recv_sem=rsem,
                    device_id=device,
                    device_id_type=MESH,
                ).start()
            self.all = pltpu.make_async_remote_copy(
                src_ref=slots.at[pl.ds(0, len(devices))],
                dst_ref=slots.at[pl.ds(0, len(devices))],
                send_sem=ssem,
                recv_sem=rsem,
                device_id=devices[0],
                device_id_type=MESH,
            )
            self.wait_recv = self.all.wait_recv
            self.wait_send = self.all.wait_send

    def ring(slots, mine, devices, ssem, rsem):
        copies = Ring(slots, mine, devices, ssem, rsem)
        pending.append(copies)
        return copies

    def reduce_grid(part, from_core, from_near, mid, first, second, total, ssem, rsem, meanwhile):
        copy = send(part.at[:, 1 - core], from_core, ssem.at[0], rsem.at[0], sibling)
        copy.wait_recv()
        mid[...] = part[:, core] + from_core[...]
        copies = []
        for k, (d, e) in enumerate(group):
            to_side = 1 - side if e else side
            copies.append(
                send(mid.at[x_peer(d), to_side], from_near.at[x, side], ssem.at[k + 1], rsem.at[k + 1], near(d, e))
            )
        from_near[x, side] = mid[x, side]
        meanwhile[0]()
        for copy in copies:
            copy.wait_recv()
        value = jnp.sum(from_near[...].reshape((2 * NX,) + total.shape), axis=0)
        along_y, along_z = first
        along_y[pair] = value[:quarter]
        along_z[z] = value[quarter:]
        copies = [
            ring(along_y, pair, y_devices, ssem.at[8], rsem.at[8]),
            ring(along_z, z, z_devices, ssem.at[9], rsem.at[9]),
        ]
        meanwhile[1]()
        meanwhile[2]()
        for copy in copies:
            copy.wait_recv()
        then_z, then_y = second
        then_z[z] = jnp.sum(along_y[...], axis=0)
        then_y[pair] = jnp.sum(along_z[...], axis=0)
        copies = [
            ring(then_z, z, z_devices, ssem.at[10], rsem.at[10]),
            ring(then_y, pair, y_devices, ssem.at[11], rsem.at[11]),
        ]
        meanwhile[3]()
        for copy in copies:
            copy.wait_recv()
        total[:quarter] = jnp.sum(then_z[...], axis=0)
        total[quarter:] = jnp.sum(then_y[...], axis=0)

    extra = []

    def nothing():
        pass

    def gather_last():
        for e in (2, 1, 3):
            for d in range(1, NX):
                owner = lax.rem(x + e + d, NX)
                there = pl.ds(pl.multiple_of(owner * hub_cols + last, 128), piece)
                extra.append(
                    send(
                        phi_ref.at[:, there],
                        phi_last.at[d - 1, block_rows(x)],
                        last_send.at[e - 1, d - 1],
                        last_recv.at[e - 1, d - 1],
                        x_device(e),
                    )
                )

    reduce_grid(
        cpart,
        ccore,
        cx,
        cmid,
        (cfirst_y, cfirst_z),
        (csecond_z, csecond_y),
        csum,
        c_send,
        c_recv,
        (nothing, gather_last, lambda: settle(2 + (NX - 1) ** 2), nothing),
    )
    cfull[core, x, side] = csum[...]
    copies = []
    for k, (d, e) in enumerate(group):
        copies.append(
            send(csum, cfull.at[core, x, side], c_send.at[12 + k], c_recv.at[12 + k], near(d, e))
        )
    passed = []
    for d in (0, 1, 3, 2):
        for (distance, _), copy in zip(group, copies):
            if distance == d:
                copy.wait_recv()
        origin = lax.rem(x + NX - d, NX)
        passed.append(
            send(cfull.at[core, origin], cfull.at[core, origin], c_send.at[20 + d], c_recv.at[20 + d], sibling)
        )
    for copy in passed:
        copy.wait_recv()

    def rows_of(a):
        return [cfull[c, a].reshape(half, NX * block) for c in range(2)]

    coefficients = jnp.concatenate(
        [part for a in range(NX) for part in rows_of(a)], axis=0
    )

    returns, own = [], []

    def give_back(index):
        here = pl.ds(index * piece, piece)
        mine = pl.ds(pl.multiple_of(x * hub_cols + index * piece, 128), piece)
        for d in (2, 1, 3):
            returns.append(
                send(
                    rb.at[block_rows(x_peer(d)), here],
                    res_ref.at[:, mine],
                    out_send.at[index, d - 1],
                    out_recv.at[index, d - 1],
                    x_device(d),
                )
            )

    sent = 0
    same = cross = None
    width = hub_cols // PARTS
    for k in range(PARTS):
        here = pl.ds(k * width, width)
        residual = sb[:, here] - product(coefficients, phib[:, here], 0)
        rb[:, here] = residual
        while sent < EARLY and (sent + 1) * piece <= (k + 1) * width:
            give_back(sent)
            sent += 1
        high = residual.astype(jnp.bfloat16)
        low = (residual - high.astype(jnp.float32)).astype(jnp.bfloat16)
        high_high = plain_product(high, high)
        high_low = plain_product(high, low)
        same = high_high if same is None else same + high_high
        cross = high_low if cross is None else cross + high_low
    gpart[...] = (same + (cross + cross.T)).reshape(gpart.shape)

    def send_some():
        for index in range(EARLY, MIDDLE):
            give_back(index)

    def send_the_rest():
        mine = pl.ds(pl.multiple_of(x * hub_cols, 128), hub_cols)
        copy = pltpu.make_async_copy(rb.at[block_rows(x)], res_ref.at[:, mine], out_own)
        copy.start()
        own.append(copy)
        for index in range(MIDDLE, PIECES - 1):
            give_back(index)

    def own_residual():
        for copy in extra_own:
            copy.wait()
        for copy in extra:
            copy.wait_recv()
        mine = jnp.concatenate(rows_of(x), axis=0)
        coef_ref[...] = mine
        for d in range(1, NX):
            there = pl.ds(pl.multiple_of(x_peer(d) * hub_cols + last, 128), piece)
            res_ref[:, there] = s_last[d - 1] - product(mine, phi_last[d - 1], 0)

    later = (NX - 1) * (PIECES - 1) + 2

    reduce_grid(
        gpart,
        gcore,
        gx,
        gmid,
        (gfirst_y, gfirst_z),
        (gsecond_z, gsecond_y),
        gsum,
        g_send,
        g_recv,
        (send_some, send_the_rest, own_residual, lambda: settle(later + 2)),
    )
    gpair[core, side] = gsum[...]
    copies = []
    for k, partner in enumerate((near(0, 1, 1), near(0, 1), sibling)):
        copies.append(send(gpair.at[core, side], gpair.at[core, side], g_send.at[12 + k], g_recv.at[12 + k], partner))
    for done in returns:
        done.wait_recv()
    for done in own:
        done.wait()
    settle(3)
    for copy in copies:
        copy.wait_recv()
    gram = gpair[...].reshape(block, NX * block) / total_rows
    gram_ref[...] = gram
    column = lax.broadcasted_iota(jnp.int32, gram.shape, 1)
    row = lax.broadcasted_iota(jnp.int32, gram.shape, 0)
    diagonal = jnp.sum(jnp.where(column == row + x * block, gram, 0.0), axis=0, keepdims=True)
    diagonal = functools.reduce(jnp.add, [diagonal[:, a * block : (a + 1) * block] for a in range(NX)])
    norm_ref[...] = jnp.sqrt(diagonal)

    settle(0)


def copy_kernel(*refs):
    n = (len(refs) - 1) // 2
    sems = refs[-1]
    copies = [pltpu.make_async_copy(refs[i], refs[n + i], sems.at[i]) for i in range(n)]
    for copy in copies:
        copy.start()
    for copy in copies:
        copy.wait()


def copied(arrays):
    hbm = pl.BlockSpec(memory_space=pltpu.HBM)
    vmem = pl.BlockSpec(memory_space=pltpu.VMEM)
    return pl.pallas_call(
        copy_kernel,
        out_shape=tuple(jax.ShapeDtypeStruct(a.shape, a.dtype) for a in arrays),
        in_specs=[vmem] * len(arrays),
        out_specs=(hbm,) * len(arrays),
        scratch_shapes=[pltpu.SemaphoreType.DMA((len(arrays),))],
        compiler_params=pltpu.CompilerParams(vmem_limit_bytes=1024 * 1024),
    )(*arrays)


def per_device(modes_basis, snapshots):
    block, local_cols = modes_basis.shape
    size = block * NX
    hub_cols = local_cols // NX
    share = block // 4
    total_rows = local_cols * lax.axis_size("rows")
    f32 = jnp.float32
    sems = 24
    hbm = pl.BlockSpec(memory_space=pltpu.HBM)
    vmem = pl.BlockSpec(memory_space=pltpu.VMEM)
    part = pltpu.VMEM((NX, 2, 2, share, size), f32)
    near = pltpu.VMEM((NX, 2, share, size), f32)
    rings = [pltpu.VMEM((n, share // 2, size), f32) for n in (NY // 2, NZ, NY // 2, NZ)]
    own = pltpu.VMEM((share, size), f32)
    outs = pl.pallas_call(
        functools.partial(kernel, float(total_rows)),
        out_shape=(
            pltpu.VMEM((block, size), f32),
            pltpu.VMEM((block, local_cols), f32),
            pltpu.VMEM((block, size), f32),
            pltpu.VMEM((1, block), f32),
        ),
        in_specs=[hbm, hbm],
        out_specs=(vmem, vmem, vmem, vmem),
        scratch_shapes=[
            pltpu.VMEM((size, hub_cols), f32),
            pltpu.VMEM((size, hub_cols), f32),
            pltpu.VMEM((size, hub_cols), f32),
            part,
            near,
            near,
            *rings,
            pltpu.VMEM((2, NX, 2, share, size), f32),
            part,
            near,
            near,
            *rings,
            pltpu.VMEM((2, 2, share, size), f32),
            own,
            own,
            near,
            near,
            pltpu.SemaphoreType.DMA((CHUNKS, 2, NX - 1)),
            pltpu.SemaphoreType.DMA((CHUNKS, 2, NX - 1)),
            pltpu.SemaphoreType.DMA((CHUNKS, 2)),
            pltpu.SemaphoreType.DMA((sems,)),
            pltpu.SemaphoreType.DMA((sems,)),
            pltpu.SemaphoreType.DMA((sems,)),
            pltpu.SemaphoreType.DMA((sems,)),
            pltpu.SemaphoreType.DMA((PIECES, NX - 1)),
            pltpu.SemaphoreType.DMA((PIECES, NX - 1)),
            pltpu.SemaphoreType.DMA,
            pltpu.VMEM((NX - 1, size, hub_cols // PIECES), f32),
            pltpu.VMEM((NX - 1, block, hub_cols // PIECES), f32),
            pltpu.SemaphoreType.DMA((NX - 1, NX - 1)),
            pltpu.SemaphoreType.DMA((NX - 1, NX - 1)),
            pltpu.SemaphoreType.DMA((2, NX - 1)),
        ],
        compiler_params=pltpu.CompilerParams(
            collective_id=0, has_side_effects=True, vmem_limit_bytes=56 * 1024 * 1024
        ),
        cost_estimate=pl.CostEstimate(
            flops=6 * size * size * hub_cols, bytes_accessed=12 * block * local_cols, transcendentals=0
        ),
    )(modes_basis, snapshots)
    coefficients, residual, gram, norm = copied(outs)
    return coefficients, residual, gram, norm.reshape(block)


def solution(mesh):
    in_specs = (P("modes", "rows"), P("modes", "rows"))
    out_specs = (P("modes", None), P("modes", "rows"), P("modes", None), P("modes"))
    return jax.shard_map(
        per_device, mesh=mesh, in_specs=in_specs, out_specs=out_specs, check_vma=False
    )
```
